32 devices in a mesh: elem: 16 (over z, x, core), lev: 2 (over y).
Axes of the slice: x: 2, y: 2, z: 4, core: 2. Of those that a mesh axis runs over, the one named last changes fastest.
Arguments:
- zonal_wind: float32 [128, 16, 2048], P('lev', None, 'elem'), may hold values from -6 to 6
- meridional_wind: float32 [128, 16, 2048], P('lev', None, 'elem'), may hold values from -6 to 6
- vertical_wind: float32 [128, 16, 2048], P('lev', None, 'elem'), may hold values from -6 to 6
- pressure: float32 [128, 16, 2048], P('lev', None, 'elem'), may hold values from -6 to 6
- geopotential: float32 [128, 16, 2048], P('lev', None, 'elem'), may hold values from -6 to 6
- layer_mass: float32 [128, 16, 2048], P('lev', None, 'elem'), may hold values from 0.5 to 2
- stiffness: float32 [128, 16, 2048], P(None, 'lev', 'elem'), may hold values from 4 to 1024
- elem_order: int32 [16, 128], P('elem'), may hold values from 0 to 127, each once within a row
Outputs:
- zonal_out: float32 [128, 16, 2048], P('lev', None, 'elem')
- meridional_out: float32 [128, 16, 2048], P('lev', None, 'elem')
- vertical_out: float32 [128, 16, 2048], P('lev', None, 'elem')
- pressure_out: float32 [128, 16, 2048], P('lev', None, 'elem')
- geopotential_out: float32 [128, 16, 2048], P('lev', None, 'elem')
The draws below stay inside these ranges and needn't reach their ends.
Inputs may be any that keep to these rules, and one draw needn't show every extreme that they name: `elem_order`: each row is a permutation of the positions 0 .. 127 of its strip.
All inputs are finite; a program needn't handle non-finite values.
Results may differ from the reference program's by a relative error of at most 0.0003.
Values sent between devices are 32-bit elements; how exact they have to be, the bound alone decides.
A program may use at most 128 MiB of HBM per device.

```python
import math
import jax
import jax.numpy as jnp
import numpy as np
from jax import lax

NLEV = 128
NODES = 16
SUBSTEPS = 3
EY = 128
STRIPS = 16
NELEM = 2048


def steps_of(own_key, dims, pieces, smallest, top_value):
    def one(position, shards_of):
        draws = jax.random.uniform(jax.random.fold_in(jax.random.fold_in(own_key, 6), position), (shards_of,), jnp.float32, smallest / len(pieces), top_value / len(pieces))
        return jnp.repeat(jnp.exp(draws), dims[position] // shards_of).reshape((-1,) + (1,) * (len(dims) - position - 1))

    level = one(*pieces[0])
    for cut in pieces[1:]:
        level = level * one(*cut)
    return level


def normal_values(stream_key, shape, deviation, bound, split=(), kind=jnp.bfloat16):
    entries = deviation * jax.random.normal(stream_key, shape, jnp.float32)
    if split:
        entries = entries * steps_of(stream_key, shape, split, -0.22, 0.18)
    return jnp.clip(entries, -bound, bound).astype(kind)


def setup_inputs(seed: int = 0) -> dict:
    streams_of = jax.random.split(jax.random.key(seed), 9)
    return {
        "zonal_wind": normal_values(streams_of[0], (NLEV, NODES, NELEM), 1.0, 6.0, ((0, 2), (2, 16)), jnp.float32),
        "meridional_wind": normal_values(streams_of[1], (NLEV, NODES, NELEM), 1.0, 6.0, ((0, 2), (2, 16)), jnp.float32),
        "vertical_wind": normal_values(streams_of[2], (NLEV, NODES, NELEM), 1.0, 6.0, ((0, 2), (2, 16)), jnp.float32),
        "pressure": normal_values(streams_of[3], (NLEV, NODES, NELEM), 1.0, 6.0, ((0, 2), (2, 16)), jnp.float32),
        "geopotential": normal_values(streams_of[4], (NLEV, NODES, NELEM), 1.0, 6.0, ((0, 2), (2, 16)), jnp.float32),
        "layer_mass": jnp.clip(jnp.exp(math.log(2.0) - 1.3862944 * jax.random.uniform(streams_of[5], (NLEV, NODES, NELEM), jnp.float32) ** steps_of(streams_of[5], (NLEV, NODES, NELEM), ((0, 2), (2, 16)), -0.2, 0.2)), 0.5, 2.0),
        "stiffness": jnp.clip(jnp.exp(math.log(1024.0) - 5.5451774 * jax.random.uniform(streams_of[6], (NLEV, NODES, NELEM), jnp.float32) ** steps_of(streams_of[6], (NLEV, NODES, NELEM), ((1, 2), (2, 16)), -0.2, 0.2)), 4.0, 1024.0),
        "elem_order": jax.vmap(lambda own: jax.random.permutation(own, EY))(jax.random.split(streams_of[7], STRIPS)).reshape((STRIPS, EY)).astype(jnp.int32),
    }


horizontal_speed = 0.12
drift_first = 0.1
drift_second = 0.06
geopotential_rate = 2.0

def gll_tables():
    points = np.array([-1.0, -1.0 / math.sqrt(5.0), 1.0 / math.sqrt(5.0), 1.0])
    quadrature = np.array([1.0 / 6.0, 5.0 / 6.0, 5.0 / 6.0, 1.0 / 6.0])
    derivative = np.zeros((4, 4))
    for target in range(4):
        for source in range(4):
            if target == source:
                derivative[target, source] = sum((1.0 / (points[target] - points[other]) for other in range(4) if other != target))
            else:
                top_term = math.prod((points[target] - points[other] for other in range(4) if other != target))
                low_term = math.prod((points[source] - points[other] for other in range(4) if other != source))
                derivative[target, source] = top_term / (low_term * (points[target] - points[source]))
    return (jnp.asarray(derivative), jnp.asarray(np.outer(quadrature, quadrature).reshape(16)))

def along_first(field, derivative):
    return jnp.einsum('ai,lijxy->lajxy', derivative, field, precision=lax.Precision.HIGHEST)

def along_second(field, derivative):
    return jnp.einsum('aj,lijxy->liaxy', derivative, field, precision=lax.Precision.HIGHEST)

def assemble(field):
    summed = field[:, 3] + jnp.roll(field[:, 0], -1, axis=2)
    field = jnp.concatenate([jnp.roll(summed, 1, axis=2)[:, None], field[:, 1:3], summed[:, None]], 1)
    summed = field[:, :, 3] + jnp.roll(field[:, :, 0], -1, axis=3)
    return jnp.concatenate([jnp.roll(summed, 1, axis=3)[:, :, None], field[:, :, 1:3], summed[:, :, None]], 2)

def reference(zonal_wind, meridional_wind, vertical_wind, pressure, geopotential, layer_mass, stiffness, elem_order):
    derivative, weights = gll_tables()
    inverse = jnp.argsort(elem_order, axis=1).astype(jnp.int32)
    strip_base = (jnp.arange(STRIPS, dtype=jnp.int32) * EY)[:, None]
    grid_index = (strip_base + inverse).reshape(-1)
    store_index = (strip_base + elem_order).reshape(-1)

    def to_grid(field):
        return jnp.take(field, grid_index, axis=2).reshape(field.shape[0], 4, 4, STRIPS, EY)

    def to_store(field):
        return jnp.take(field.reshape(NLEV, 16, NELEM), store_index, axis=2)
    mass = to_grid(layer_mass * weights[None, :, None])
    recip = 1.0 / assemble(mass)
    coeff = to_grid(stiffness)
    root = jnp.sqrt(coeff)
    coeff_last = jnp.moveaxis(coeff, 0, -1)
    zero_col = jnp.zeros_like(coeff_last[..., :1])
    lower = jnp.concatenate([zero_col, -coeff_last[..., 1:]], -1)
    upper = jnp.concatenate([-coeff_last[..., :-1], zero_col], -1)
    middle = 1.0 + 2.0 * coeff_last
    zonal = to_grid(zonal_wind)
    meridional = to_grid(meridional_wind)
    upward = to_grid(vertical_wind)
    press = to_grid(pressure)
    geopot = to_grid(geopotential)
    widths = ((1, 1), (0, 0), (0, 0), (0, 0), (0, 0))
    for step in range(SUBSTEPS):
        new_zonal = zonal + recip * assemble(mass * (-horizontal_speed * along_first(press, derivative)))
        new_merid = meridional + recip * assemble(mass * (-horizontal_speed * along_second(press, derivative)))
        new_upward = upward + recip * assemble(mass * -(drift_first * along_first(upward, derivative) + drift_second * along_second(upward, derivative)))
        new_geopot = geopot + recip * assemble(mass * -(drift_first * along_first(geopot, derivative) + drift_second * along_second(geopot, derivative)))
        zonal, meridional, upward, geopot = (new_zonal, new_merid, new_upward, new_geopot)
        divergence = along_first(zonal, derivative) + along_second(meridional, derivative)
        press = press + recip * assemble(mass * (-horizontal_speed * divergence))
        padded = jnp.pad(press, widths)
        rhs = upward - root * 0.5 * (padded[2:] - padded[:-2])
        solved = lax.linalg.tridiagonal_solve(lower, middle, upper, jnp.moveaxis(rhs, 0, -1)[..., None])[..., 0]
        solved = jnp.moveaxis(solved, -1, 0)
        padded = jnp.pad(solved, widths)
        press = press - root * 0.5 * (padded[2:] - padded[:-2])
        geopot = geopot + geopotential_rate * solved
        upward = solved
    return (to_store(zonal), to_store(meridional), to_store(upward), to_store(press), to_store(geopot))
```

```python
import functools
import math

import jax
import jax.numpy as jnp
import numpy as np
from jax import lax
from jax.experimental import pallas as pl
from jax.experimental.pallas import tpu as pltpu
from jax.sharding import PartitionSpec as P

SUBSTEPS = 3


horizontal_speed = 0.12
drift_first = 0.1
drift_second = 0.06
geopotential_rate = 2.0


def padded(cells, sides, width):
    for axis, dim in sides:
        count = lax.axis_size(axis)
        head = lax.slice_in_dim(cells, 0, width, axis=dim)
        tail = lax.slice_in_dim(cells, cells.shape[dim] - width, cells.shape[dim], axis=dim)
        cells = jnp.concatenate(
            [
                lax.ppermute(tail, axis, [(i, (i + 1) % count) for i in range(count)]),
                cells,
                lax.ppermute(head, axis, [((i + 1) % count, i) for i in range(count)]),
            ],
            axis=dim,
        )
    return cells


def gll_tables():
    points = np.array([-1.0, -1.0 / math.sqrt(5.0), 1.0 / math.sqrt(5.0), 1.0])
    quadrature = np.array([1.0 / 6.0, 5.0 / 6.0, 5.0 / 6.0, 1.0 / 6.0])
    derivative = np.zeros((4, 4))
    for target in range(4):
        for source in range(4):
            if target == source:
                derivative[target, source] = sum(
                    (
                        1.0 / (points[target] - points[other])
                        for other in range(4)
                        if other != target
                    )
                )
            else:
                top_term = math.prod(
                    (points[target] - points[other] for other in range(4) if other != target)
                )
                low_term = math.prod(
                    (points[source] - points[other] for other in range(4) if other != source)
                )
                derivative[target, source] = top_term / (
                    low_term * (points[target] - points[source])
                )
    return (
        jnp.asarray(derivative, jnp.float32),
        jnp.asarray(np.outer(quadrature, quadrature).reshape(16), jnp.float32),
    )


def derivative_along(field, letters, which, derivative):
    result = letters.replace(which, "a")
    return jnp.einsum(
        "a" + which + "," + letters + "->" + result,
        derivative,
        field,
        precision=lax.Precision.HIGHEST,
    )


def assemble(stacked):
    axis_i, axis_j, axis_y = (2, 3, 4)
    left = lax.index_in_dim(stacked, 0, axis_i, keepdims=False)
    right = lax.index_in_dim(stacked, 3, axis_i, keepdims=False)
    faces = jnp.stack([left, right], 0)
    extended = padded(faces, (("elem", 0),), 1)
    left = left + extended[0]
    right = right + extended[3]
    stacked = jnp.concatenate(
        [
            jnp.expand_dims(left, axis_i),
            lax.slice_in_dim(stacked, 1, 3, axis=axis_i),
            jnp.expand_dims(right, axis_i),
        ],
        axis_i,
    )
    lower = lax.index_in_dim(stacked, 0, axis_j, keepdims=False)
    upper = lax.index_in_dim(stacked, 3, axis_j, keepdims=False)
    faces = jnp.stack([lower, upper], 0)
    length = faces.shape[axis_y]
    extended = jnp.concatenate(
        [
            lax.slice_in_dim(faces, length - 1, length, axis=axis_y),
            faces,
            lax.slice_in_dim(faces, 0, 1, axis=axis_y),
        ],
        axis_y,
    )
    lower = lower + lax.slice_in_dim(extended[1], 0, length, axis=axis_y - 1)
    upper = upper + lax.slice_in_dim(extended[0], 2, length + 2, axis=axis_y - 1)
    return jnp.concatenate(
        [
            jnp.expand_dims(lower, axis_j),
            lax.slice_in_dim(stacked, 1, 3, axis=axis_j),
            jnp.expand_dims(upper, axis_j),
        ],
        axis_j,
    )


def lift(field, stride, axis, fill):
    length = field.shape[axis]
    kept = lax.slice_in_dim(field, stride, length, axis=axis)
    padding = jnp.full_like(lax.slice_in_dim(field, 0, stride, axis=axis), fill)
    return jnp.concatenate([kept, padding], axis)


def sink(field, stride, axis, fill):
    length = field.shape[axis]
    kept = lax.slice_in_dim(field, 0, length - stride, axis=axis)
    padding = jnp.full_like(lax.slice_in_dim(field, 0, stride, axis=axis), fill)
    return jnp.concatenate([padding, kept], axis)


def column_step(upward, press, coeff, root, axis):
    rhs = upward - root * 0.5 * (lift(press, 1, axis, 0.0) - sink(press, 1, axis, 0.0))
    lower = -coeff
    upper = -coeff
    middle = 1.0 + 2.0 * coeff
    length = coeff.shape[axis]
    stride = 1
    while stride < length:
        from_below = -lower / sink(middle, stride, axis, 1.0)
        from_above = -upper / lift(middle, stride, axis, 1.0)
        new_lower = from_below * sink(lower, stride, axis, 0.0)
        new_upper = from_above * lift(upper, stride, axis, 0.0)
        middle = (
            middle
            + from_below * sink(upper, stride, axis, 0.0)
            + from_above * lift(lower, stride, axis, 0.0)
        )
        rhs = (
            rhs
            + from_below * sink(rhs, stride, axis, 0.0)
            + from_above * lift(rhs, stride, axis, 0.0)
        )
        lower, upper = (new_lower, new_upper)
        stride = stride * 2
    solved = rhs / middle
    press = press - root * 0.5 * (lift(solved, 1, axis, 0.0) - sink(solved, 1, axis, 0.0))
    return (solved, press)


def substep(state, mass, recip, letters, derivative, vertical):
    zonal, meridional, upward, press, geopot = state
    tendencies = jnp.stack(
        [
            mass * (-horizontal_speed * derivative_along(press, letters, "i", derivative)),
            mass * (-horizontal_speed * derivative_along(press, letters, "j", derivative)),
            mass
            * -(
                drift_first * derivative_along(upward, letters, "i", derivative)
                + drift_second * derivative_along(upward, letters, "j", derivative)
            ),
            mass
            * -(
                drift_first * derivative_along(geopot, letters, "i", derivative)
                + drift_second * derivative_along(geopot, letters, "j", derivative)
            ),
        ],
        0,
    )
    summed = assemble(tendencies)
    zonal = zonal + recip * summed[0]
    meridional = meridional + recip * summed[1]
    upward = upward + recip * summed[2]
    geopot = geopot + recip * summed[3]
    divergence = derivative_along(zonal, letters, "i", derivative) + derivative_along(
        meridional, letters, "j", derivative
    )
    press = press + recip * assemble(jnp.expand_dims(mass * (-horizontal_speed * divergence), 0))[0]
    solved, press = vertical(upward, press)
    geopot = geopot + geopotential_rate * solved
    return (zonal, meridional, solved, press, geopot)


def body(
    zonal_wind,
    meridional_wind,
    vertical_wind,
    pressure,
    geopotential,
    layer_mass,
    stiffness,
    elem_order,
):
    derivative, weights = gll_tables()
    order = elem_order[0]
    length = order.shape[0]
    inverse = jnp.zeros((length,), jnp.int32).at[order].set(jnp.arange(length, dtype=jnp.int32))
    levels = zonal_wind.shape[0]
    fields = [
        jnp.take(field, inverse, axis=2)
        for field in (zonal_wind, meridional_wind, vertical_wind, pressure, geopotential)
    ]
    mass = jnp.take(layer_mass, inverse, axis=2) * weights[None, :, None]
    coeff_grid = jnp.take(stiffness, inverse, axis=2)
    grid_mass = mass.reshape(levels, 4, 4, length)
    recip = 1.0 / assemble(jnp.expand_dims(grid_mass, 0))[0]
    root_grid = jnp.sqrt(coeff_grid)

    def vertical(upward, press):
        stacked = jnp.stack([upward, press], 0).reshape(2, levels, 16, length)
        columns = lax.all_to_all(stacked, "lev", split_axis=2, concat_axis=1, tiled=True)
        solved, press_new = column_step(columns[0], columns[1], coeff_grid, root_grid, 0)
        back = lax.all_to_all(
            jnp.stack([solved, press_new], 0), "lev", split_axis=1, concat_axis=2, tiled=True
        )
        back = back.reshape(2, levels, 4, 4, length)
        return (back[0], back[1])

    state = tuple((field.reshape(levels, 4, 4, length) for field in fields))
    for step in range(SUBSTEPS):
        state = substep(state, grid_mass, recip, "lijy", derivative, vertical)
    results = [field.reshape(levels, 16, length) for field in state]
    outputs = [jnp.take(field, order, axis=2) for field in results]
    return (outputs[0], outputs[1], outputs[2], outputs[3], outputs[4])


CHUNKS = 2
TILE = 8


def derivative_parts():
    points = np.array([-1.0, -1.0 / math.sqrt(5.0), 1.0 / math.sqrt(5.0), 1.0])
    matrix = np.zeros((4, 4))
    for a in range(4):
        for b in range(4):
            if a == b:
                matrix[a, b] = sum(1.0 / (points[a] - points[o]) for o in range(4) if o != a)
            else:
                top = math.prod(points[a] - points[o] for o in range(4) if o != a)
                low = math.prod(points[b] - points[o] for o in range(4) if o != b)
                matrix[a, b] = top / (low * (points[a] - points[b]))
    return matrix


MATRIX = derivative_parts()


def line(f0, f1, f2, f3, scale):
    outer, inner = f0 - f3, f1 - f2
    bend = (f0 + f3) - (f1 + f2)
    out = [None] * 4
    for a in (0, 1):
        m = MATRIX[a] * scale
        odd = float(0.5 * (m[0] - m[3])) * outer + float(0.5 * (m[1] - m[2])) * inner
        even = float(0.5 * (m[0] + m[3])) * bend
        out[a], out[3 - a] = odd + even, odd - even
    return out


def along_i(f, scale):
    out = [None] * 16
    for j in range(4):
        for i, value in enumerate(line(f[j], f[4 + j], f[8 + j], f[12 + j], scale)):
            out[4 * i + j] = value
    return out


def along_j(f, scale):
    out = [None] * 16
    for i in range(4):
        out[4 * i : 4 * i + 4] = line(*f[4 * i : 4 * i + 4], scale)
    return out


def ahead(x):
    return pltpu.roll(x, x.shape[1] - 1, 1)


def behind(x):
    return pltpu.roll(x, 1, 1)


def join_j(f):
    out = list(f)
    for i in range(4):
        shared = f[4 * i + 3] + ahead(f[4 * i])
        out[4 * i + 3] = shared
        out[4 * i] = behind(shared)
    return out


def lanes(x, index):
    return jnp.take_along_axis(x, index, axis=1, mode="promise_in_bounds")


def fused(
    strips,
    zon, mer, ver, pre, geo, lay, stf, inv_ref, ord_ref,
    o_zon, o_mer, o_ver, o_pre, o_geo,
    U, V, G, M, R, P, W, Z, C, I, H, A,
    s_m, r_m, s_uv, r_uv, s_w, r_w, s_d, r_d, s_g, r_g, s_e, r_e, r_a,
    send_sem, recv_sem,
):
    levels = U.shape[1]
    span = levels // CHUNKS
    tiles = span // TILE
    me = lax.axis_index("elem")
    lev = lax.axis_index("lev")
    left, right = lax.rem(me + strips - 1, strips), lax.rem(me + 1, strips)
    other = 1 - lev
    inv = inv_ref[...]
    order = ord_ref[...]
    quad = [1.0 / 6.0, 5.0 / 6.0, 5.0 / 6.0, 1.0 / 6.0]
    weights = [quad[n // 4] * quad[n % 4] for n in range(16)]
    started = []
    MESH = pl.DeviceIdType.MESH

    def send(src, dst, target):
        slot = len(started)
        copy = pltpu.make_async_remote_copy(
            src_ref=src, dst_ref=dst, send_sem=send_sem.at[slot], recv_sem=recv_sem.at[slot],
            device_id=target, device_id_type=MESH,
        )
        copy.start()
        started.append(copy)
        return copy

    def send_faces(out, back, step, c):
        return [
            send(out.at[step, 0, c], back.at[step, 0, c], {"elem": left}),
            send(out.at[step, 1, c], back.at[step, 1, c], {"elem": right}),
        ]

    def arrive(copies):
        for copy in copies:
            copy.wait_recv()

    def column_rows(n, l0):
        return (pl.ds(l0 * 16 + n, TILE, stride=16), slice(None))

    def node_rows(n, l0):
        return (n, pl.ds(l0, TILE), slice(None))

    def each_tile(c, work):
        def go(b, carry):
            work(pl.multiple_of(c * span + b * TILE, TILE), pl.multiple_of(b * TILE, TILE))
            return carry

        lax.fori_loop(0, tiles, go, 0)

    def put_faces(buf, step, c, at, b0, f):
        for j in range(3):
            buf[step, 0, c, at + j, pl.ds(b0, TILE), :] = f[j]
            buf[step, 1, c, at + j, pl.ds(b0, TILE), :] = f[12 + j]

    def total_faces(out, back, step, c, at, b0):
        result = {}
        for i, own, theirs in ((0, 0, 1), (3, 1, 0)):
            for j in range(3):
                result[4 * i + j] = (
                    out[step, own, c, at + j, pl.ds(b0, TILE), :]
                    + back[step, theirs, c, at + j, pl.ds(b0, TILE), :]
                )
            result[4 * i + 3] = ahead(result[4 * i])
        return result

    barrier = pltpu.get_barrier_semaphore()
    for target in ({"elem": left}, {"elem": right}, {"lev": other}):
        pl.semaphore_signal(barrier, inc=1, device_id=target, device_id_type=MESH)
    pl.semaphore_wait(barrier, 3)

    stiff_copy = send(stf.at[pl.ds(pl.multiple_of(other * levels, 8), levels)], r_a, {"lev": other})

    def gather_rows(src, dst, c):
        def go(b, carry):
            for q in range(16):
                at = pl.ds(pl.multiple_of(c * span * 16 + b * 128 + q * 8, 8), 8)
                dst[at, :] = lanes(src[at, :], inv)
            return carry

        lax.fori_loop(0, tiles, go, 0)

    def load_mass(c):
        def work(l0, b0):
            m = [lanes(lay[column_rows(n, l0)], inv) * weights[n] for n in range(16)]
            for n in range(16):
                M[node_rows(n, l0)] = m[n]
            m = join_j(m)
            for n in range(4, 12):
                R[node_rows(n, l0)] = 1.0 / m[n]
            put_faces(s_m, 0, c, 0, b0, m)

        each_tile(c, work)

    def wind_step(step, c):
        def work(l0, b0):
            p = [P[column_rows(n, l0)] for n in range(16)]
            m = [M[node_rows(n, l0)] for n in range(16)]
            for at, field, d in ((0, U, along_i), (3, V, along_j)):
                t = join_j([x * y for x, y in zip(m, d(p, -horizontal_speed))])
                for n in range(4, 12):
                    add = R[node_rows(n, l0)] * t[n]
                    field[node_rows(n, l0)] = add if step == 0 else field[node_rows(n, l0)] + add
                put_faces(s_uv, step, c, at, b0, t)

        each_tile(c, work)

    def start_winds(c):
        def work(l0, b0):
            for src, field in ((zon, U), (mer, V)):
                for n in range(16):
                    value = lanes(src[column_rows(n, l0)], inv)
                    if 4 <= n < 12:
                        value = value + field[node_rows(n, l0)]
                    field[node_rows(n, l0)] = value

        each_tile(c, work)

    def drift(f, m):
        first, second = along_i(f, -drift_first), along_j(f, -drift_second)
        return join_j([k * (x + y) for k, x, y in zip(m, first, second)])

    def vertical_step(step, c):
        def work(l0, b0):
            m = [M[node_rows(n, l0)] for n in range(16)]
            w = [W[column_rows(n, l0)] for n in range(16)]
            for n in range(16):
                if step == 0:
                    G[node_rows(n, l0)] = lanes(geo[column_rows(n, l0)], inv)
                else:
                    G[node_rows(n, l0)] = G[node_rows(n, l0)] + geopotential_rate * w[n]
            t = drift(w, m)
            for n in range(4, 12):
                W[column_rows(n, l0)] = w[n] + R[node_rows(n, l0)] * t[n]
            put_faces(s_w, step, c, 0, b0, t)

        each_tile(c, work)

    def geopotential_step(step, c):
        def work(l0, b0):
            m = [M[node_rows(n, l0)] for n in range(16)]
            g = [G[node_rows(n, l0)] for n in range(16)]
            t = drift(g, m)
            for n in range(4, 12):
                G[node_rows(n, l0)] = g[n] + R[node_rows(n, l0)] * t[n]
            put_faces(s_g, step, c, 0, b0, t)

        each_tile(c, work)

    def mass_faces(c):
        def work(l0, b0):
            for n, total in total_faces(s_m, r_m, 0, c, 0, b0).items():
                R[node_rows(n, l0)] = 1.0 / total

        each_tile(c, work)

    def divergence_step(step, c):
        def work(l0, b0):
            for at, field in ((0, U), (3, V)):
                for n, total in total_faces(s_uv, r_uv, step, c, at, b0).items():
                    field[node_rows(n, l0)] = field[node_rows(n, l0)] + R[node_rows(n, l0)] * total
            m = [M[node_rows(n, l0)] for n in range(16)]
            du = along_i([U[node_rows(n, l0)] for n in range(16)], -horizontal_speed)
            dv = along_j([V[node_rows(n, l0)] for n in range(16)], -horizontal_speed)
            t = join_j([k * (x + y) for k, x, y in zip(m, du, dv)])
            for n in range(4, 12):
                P[column_rows(n, l0)] = P[column_rows(n, l0)] + R[node_rows(n, l0)] * t[n]
            put_faces(s_d, step, c, 0, b0, t)

        each_tile(c, work)

    def column_faces(field, out, back, step, c):
        def work(l0, b0):
            for n, total in total_faces(out, back, step, c, 0, b0).items():
                field[column_rows(n, l0)] = field[column_rows(n, l0)] + R[node_rows(n, l0)] * total

        each_tile(c, work)

    def geopotential_faces(step, c):
        def work(l0, b0):
            for n, total in total_faces(s_g, r_g, step, c, 0, b0).items():
                G[node_rows(n, l0)] = G[node_rows(n, l0)] + R[node_rows(n, l0)] * total

        each_tile(c, work)

    def row(e):
        k = e + lev * (levels - 1 - 2 * e)
        return pl.ds(pl.multiple_of(k * 16, 16), 16)

    side = (1 - 2 * lev).astype(jnp.float32)
    zero = jnp.zeros((16, P.shape[1]), jnp.float32)

    def factor():
        def fill(k, carry):
            mine = lanes(stf[lev * levels + k], inv)
            theirs = lanes(r_a[k], inv)
            top = jnp.where(lev == 0, mine, theirs)
            bottom = jnp.where(lev == 0, theirs, mine)
            both = jnp.concatenate([top, bottom], 0)
            at = pl.ds(pl.multiple_of(k * 16, 16), 16)
            A[at, :] = both
            H[at, :] = jnp.sqrt(both) * (0.5 * side)
            return carry

        lax.fori_loop(0, levels, fill, 0, unroll=4)

        def go(block, ratio):
            for u in range(4):
                at = row(block * 4 + u)
                a = A[at, :]
                turn = 1.0 / (1.0 + 2.0 * a - a * ratio)
                ratio = a * turn
                C[at, :] = ratio
                I[at, :] = turn
            return ratio

        lax.fori_loop(0, levels // 4, go, zero)
        at = row(levels - 1)
        s_e[0, 0] = C[at, :]
        s_e[0, 1] = H[at, :] * I[at, :]
        return send(s_e.at[0], r_e.at[0], {"lev": other})

    def eliminate(step):
        def one(e, before, here, after, z):
            at = row(e)
            z = (W[at, :] - H[at, :] * (after - before)) * I[at, :] + C[at, :] * z
            Z[at, :] = z
            return here, after, z

        def go(block, carry):
            before, here, z = carry
            for u in range(8):
                e = block * 8 + u
                after = P[row(e + 1), :]
                before, here, z = one(e, before, here, after, z)
            return before, here, z

        carry = lax.fori_loop(0, levels // 8 - 1, go, (zero, P[row(0), :], zero))
        before, here, z = carry
        for u in range(8):
            e = levels - 8 + u
            after = P[row(e + 1), :] if u < 7 else zero
            before, here, z = one(e, before, here, after, z)
        s_e[step + 1, 0] = z
        s_e[step + 1, 1] = before
        return send(s_e.at[step + 1], r_e.at[step + 1], {"lev": other})

    def substitute(step):
        ratio, pull = s_e[0, 0], s_e[0, 1]
        ratio_other, pull_other = r_e[0, 0], r_e[0, 1]
        z = s_e[step + 1, 0] - pull * r_e[step + 1, 1]
        z_other = r_e[step + 1, 0] - pull_other * s_e[step + 1, 1]
        x = (z + ratio * z_other) / (1.0 - ratio * ratio_other)
        beyond = z_other + ratio_other * x
        W[row(levels - 1), :] = x

        def one(e, beyond, x):
            here = Z[row(e), :] + C[row(e), :] * x
            W[row(e), :] = here
            at = row(e + 1)
            P[at, :] = P[at, :] - H[at, :] * (beyond - here)
            return x, here

        carry = (beyond, x)
        for u in range(7):
            carry = one(levels - 2 - u, *carry)

        def go(block, carry):
            for u in range(8):
                carry = one(levels - 9 - block * 8 - u, *carry)
            return carry

        beyond, x = lax.fori_loop(0, levels // 8 - 1, go, carry)
        at = row(0)
        P[at, :] = P[at, :] - H[at, :] * beyond

    def write_nodes(field, out, c):
        def work(l0, b0):
            for n in range(16):
                out[column_rows(n, l0)] = lanes(field[node_rows(n, l0)], order)

        each_tile(c, work)

    def write_geopotential(c):
        def work(l0, b0):
            for n in range(16):
                value = G[node_rows(n, l0)] + geopotential_rate * W[column_rows(n, l0)]
                o_geo[column_rows(n, l0)] = lanes(value, order)

        each_tile(c, work)

    def write_rows(field, out):
        def go(b, carry):
            for q in range(16):
                at = pl.ds(pl.multiple_of(b * 128 + q * 8, 8), 8)
                out[at, :] = lanes(field[at, :], order)
            return carry

        lax.fori_loop(0, levels // TILE, go, 0)

    edge_copy = None
    for step in range(SUBSTEPS):
        uv, w, d, g, m = [], [], [], [], []
        for c in range(CHUNKS):
            if step == 0:
                load_mass(c)
                m.append(send_faces(s_m, r_m, 0, c))
                gather_rows(pre, P, c)
            wind_step(step, c)
            uv.append(send_faces(s_uv, r_uv, step, c))
        for c in range(CHUNKS):
            if step == 0:
                gather_rows(ver, W, c)
            vertical_step(step, c)
            w.append(send_faces(s_w, r_w, step, c))
        if step == 0:
            for c in range(CHUNKS):
                start_winds(c)
                arrive(m[c])
                mass_faces(c)
        for c in range(CHUNKS):
            arrive(uv[c])
            divergence_step(step, c)
            d.append(send_faces(s_d, r_d, step, c))
        for c in range(CHUNKS):
            geopotential_step(step, c)
            g.append(send_faces(s_g, r_g, step, c))
        if step == 0:
            stiff_copy.wait_recv()
            edge_copy = factor()
        if step == SUBSTEPS - 1:
            for c in range(CHUNKS):
                write_nodes(U, o_zon, c)
                write_nodes(V, o_mer, c)
        for c in range(CHUNKS):
            arrive(w[c])
            column_faces(W, s_w, r_w, step, c)
        for c in range(CHUNKS):
            arrive(d[c])
            column_faces(P, s_d, r_d, step, c)
        message = eliminate(step)
        for c in range(CHUNKS):
            arrive(g[c])
            geopotential_faces(step, c)
        if step == 0:
            edge_copy.wait_recv()
        message.wait_recv()
        substitute(step)
    for c in range(CHUNKS):
        write_geopotential(c)
    write_rows(W, o_ver)
    write_rows(P, o_pre)
    for copy in started:
        copy.wait_send()


def pair_step(
    strips, zonal_wind, meridional_wind, vertical_wind, pressure, geopotential, layer_mass,
    stiffness, elem_order,
):
    levels, nodes, length = zonal_wind.shape
    order = elem_order[0]
    slots = jnp.arange(length, dtype=jnp.int32)
    inverse = jnp.sum(jnp.where(order[:, None] == slots[None, :], slots[:, None], 0), axis=0)
    inv = jnp.broadcast_to(inverse[None, :], (TILE, length))
    back = jnp.broadcast_to(elem_order, (TILE, length))
    fields = [
        f.reshape(levels * nodes, length)
        for f in (zonal_wind, meridional_wind, vertical_wind, pressure, geopotential, layer_mass)
    ]
    span = levels // CHUNKS

    def faces(steps, count):
        return [pltpu.VMEM((steps, 2, CHUNKS, count, span, length), jnp.float32)] * 2

    node_major = pltpu.VMEM((nodes, levels, length), jnp.float32)
    level_major = pltpu.VMEM((levels * nodes, length), jnp.float32)
    edges = pltpu.VMEM((SUBSTEPS + 1, 2, nodes, length), jnp.float32)
    copies = 1 + 2 * CHUNKS + SUBSTEPS * 8 * CHUNKS + 1 + SUBSTEPS
    vmem = pl.BlockSpec(memory_space=pltpu.VMEM)
    outputs = pl.pallas_call(
        functools.partial(fused, strips),
        out_shape=[jax.ShapeDtypeStruct((levels * nodes, length), jnp.float32)] * 5,
        in_specs=[vmem] * 9,
        out_specs=[vmem] * 5,
        scratch_shapes=[node_major] * 5
        + [level_major] * 7
        + faces(1, 3)
        + faces(SUBSTEPS, 6)
        + faces(SUBSTEPS, 3)
        + faces(SUBSTEPS, 3)
        + faces(SUBSTEPS, 3)
        + [edges, edges, pltpu.VMEM((levels, nodes // 2, length), jnp.float32)]
        + [pltpu.SemaphoreType.DMA((copies,)), pltpu.SemaphoreType.DMA((copies,))],
        compiler_params=pltpu.CompilerParams(
            collective_id=0, has_side_effects=True, vmem_limit_bytes=40 * 1024 * 1024
        ),
        name="acoustic_substeps",
    )(*fields, stiffness, inv, back)
    return tuple(f.reshape(levels, nodes, length) for f in outputs)


def local_step(strips, pair, *arrays):
    levels, nodes, length = arrays[0].shape
    if pair == 2 and strips > 2 and nodes == 16 and length == 128 and levels % (CHUNKS * TILE) == 0:
        return pair_step(strips, *arrays)
    return body(*arrays)


def solution(mesh):
    placed = (
        P("lev", None, "elem"),
        P("lev", None, "elem"),
        P("lev", None, "elem"),
        P("lev", None, "elem"),
        P("lev", None, "elem"),
        P("lev", None, "elem"),
        P(None, "lev", "elem"),
        P("elem", None),
    )
    return jax.shard_map(
        functools.partial(local_step, mesh.shape["elem"], mesh.shape["lev"]),
        mesh=mesh,
        in_specs=placed,
        out_specs=(
            P("lev", None, "elem"),
            P("lev", None, "elem"),
            P("lev", None, "elem"),
            P("lev", None, "elem"),
            P("lev", None, "elem"),
        ),
        check_vma=False,
    )
```

```python
import functools
import math

import jax
import jax.numpy as jnp
import numpy as np
from jax import lax
from jax.experimental import pallas as pl
from jax.experimental.pallas import tpu as pltpu
from jax.sharding import PartitionSpec as P

SUBSTEPS = 3


horizontal_speed = 0.12
drift_first = 0.1
drift_second = 0.06
geopotential_rate = 2.0


def padded(cells, sides, width):
    for axis, dim in sides:
        count = lax.axis_size(axis)
        head = lax.slice_in_dim(cells, 0, width, axis=dim)
        tail = lax.slice_in_dim(cells, cells.shape[dim] - width, cells.shape[dim], axis=dim)
        cells = jnp.concatenate(
            [
                lax.ppermute(tail, axis, [(i, (i + 1) % count) for i in range(count)]),
                cells,
                lax.ppermute(head, axis, [((i + 1) % count, i) for i in range(count)]),
            ],
            axis=dim,
        )
    return cells


def gll_tables():
    points = np.array([-1.0, -1.0 / math.sqrt(5.0), 1.0 / math.sqrt(5.0), 1.0])
    quadrature = np.array([1.0 / 6.0, 5.0 / 6.0, 5.0 / 6.0, 1.0 / 6.0])
    derivative = np.zeros((4, 4))
    for target in range(4):
        for source in range(4):
            if target == source:
                derivative[target, source] = sum(
                    (
                        1.0 / (points[target] - points[other])
                        for other in range(4)
                        if other != target
                    )
                )
            else:
                top_term = math.prod(
                    (points[target] - points[other] for other in range(4) if other != target)
                )
                low_term = math.prod(
                    (points[source] - points[other] for other in range(4) if other != source)
                )
                derivative[target, source] = top_term / (
                    low_term * (points[target] - points[source])
                )
    return (
        jnp.asarray(derivative, jnp.float32),
        jnp.asarray(np.outer(quadrature, quadrature).reshape(16), jnp.float32),
    )


def derivative_along(field, letters, which, derivative):
    result = letters.replace(which, "a")
    return jnp.einsum(
        "a" + which + "," + letters + "->" + result,
        derivative,
        field,
        precision=lax.Precision.HIGHEST,
    )


def assemble(stacked):
    axis_i, axis_j, axis_y = (2, 3, 4)
    left = lax.index_in_dim(stacked, 0, axis_i, keepdims=False)
    right = lax.index_in_dim(stacked, 3, axis_i, keepdims=False)
    faces = jnp.stack([left, right], 0)
    extended = padded(faces, (("elem", 0),), 1)
    left = left + extended[0]
    right = right + extended[3]
    stacked = jnp.concatenate(
        [
            jnp.expand_dims(left, axis_i),
            lax.slice_in_dim(stacked, 1, 3, axis=axis_i),
            jnp.expand_dims(right, axis_i),
        ],
        axis_i,
    )
    lower = lax.index_in_dim(stacked, 0, axis_j, keepdims=False)
    upper = lax.index_in_dim(stacked, 3, axis_j, keepdims=False)
    faces = jnp.stack([lower, upper], 0)
    length = faces.shape[axis_y]
    extended = jnp.concatenate(
        [
            lax.slice_in_dim(faces, length - 1, length, axis=axis_y),
            faces,
            lax.slice_in_dim(faces, 0, 1, axis=axis_y),
        ],
        axis_y,
    )
    lower = lower + lax.slice_in_dim(extended[1], 0, length, axis=axis_y - 1)
    upper = upper + lax.slice_in_dim(extended[0], 2, length + 2, axis=axis_y - 1)
    return jnp.concatenate(
        [
            jnp.expand_dims(lower, axis_j),
            lax.slice_in_dim(stacked, 1, 3, axis=axis_j),
            jnp.expand_dims(upper, axis_j),
        ],
        axis_j,
    )


def lift(field, stride, axis, fill):
    length = field.shape[axis]
    kept = lax.slice_in_dim(field, stride, length, axis=axis)
    padding = jnp.full_like(lax.slice_in_dim(field, 0, stride, axis=axis), fill)
    return jnp.concatenate([kept, padding], axis)


def sink(field, stride, axis, fill):
    length = field.shape[axis]
    kept = lax.slice_in_dim(field, 0, length - stride, axis=axis)
    padding = jnp.full_like(lax.slice_in_dim(field, 0, stride, axis=axis), fill)
    return jnp.concatenate([padding, kept], axis)


def column_step(upward, press, coeff, root, axis):
    rhs = upward - root * 0.5 * (lift(press, 1, axis, 0.0) - sink(press, 1, axis, 0.0))
    lower = -coeff
    upper = -coeff
    middle = 1.0 + 2.0 * coeff
    length = coeff.shape[axis]
    stride = 1
    while stride < length:
        from_below = -lower / sink(middle, stride, axis, 1.0)
        from_above = -upper / lift(middle, stride, axis, 1.0)
        new_lower = from_below * sink(lower, stride, axis, 0.0)
        new_upper = from_above * lift(upper, stride, axis, 0.0)
        middle = (
            middle
            + from_below * sink(upper, stride, axis, 0.0)
            + from_above * lift(lower, stride, axis, 0.0)
        )
        rhs = (
            rhs
            + from_below * sink(rhs, stride, axis, 0.0)
            + from_above * lift(rhs, stride, axis, 0.0)
        )
        lower, upper = (new_lower, new_upper)
        stride = stride * 2
    solved = rhs / middle
    press = press - root * 0.5 * (lift(solved, 1, axis, 0.0) - sink(solved, 1, axis, 0.0))
    return (solved, press)


def substep(state, mass, recip, letters, derivative, vertical):
    zonal, meridional, upward, press, geopot = state
    tendencies = jnp.stack(
        [
            mass * (-horizontal_speed * derivative_along(press, letters, "i", derivative)),
            mass * (-horizontal_speed * derivative_along(press, letters, "j", derivative)),
            mass
            * -(
                drift_first * derivative_along(upward, letters, "i", derivative)
                + drift_second * derivative_along(upward, letters, "j", derivative)
            ),
            mass
            * -(
                drift_first * derivative_along(geopot, letters, "i", derivative)
                + drift_second * derivative_along(geopot, letters, "j", derivative)
            ),
        ],
        0,
    )
    summed = assemble(tendencies)
    zonal = zonal + recip * summed[0]
    meridional = meridional + recip * summed[1]
    upward = upward + recip * summed[2]
    geopot = geopot + recip * summed[3]
    divergence = derivative_along(zonal, letters, "i", derivative) + derivative_along(
        meridional, letters, "j", derivative
    )
    press = press + recip * assemble(jnp.expand_dims(mass * (-horizontal_speed * divergence), 0))[0]
    solved, press = vertical(upward, press)
    geopot = geopot + geopotential_rate * solved
    return (zonal, meridional, solved, press, geopot)


def body(
    zonal_wind,
    meridional_wind,
    vertical_wind,
    pressure,
    geopotential,
    layer_mass,
    stiffness,
    elem_order,
):
    derivative, weights = gll_tables()
    order = elem_order[0]
    length = order.shape[0]
    inverse = jnp.zeros((length,), jnp.int32).at[order].set(jnp.arange(length, dtype=jnp.int32))
    levels = zonal_wind.shape[0]
    fields = [
        jnp.take(field, inverse, axis=2)
        for field in (zonal_wind, meridional_wind, vertical_wind, pressure, geopotential)
    ]
    mass = jnp.take(layer_mass, inverse, axis=2) * weights[None, :, None]
    coeff_grid = jnp.take(stiffness, inverse, axis=2)
    grid_mass = mass.reshape(levels, 4, 4, length)
    recip = 1.0 / assemble(jnp.expand_dims(grid_mass, 0))[0]
    root_grid = jnp.sqrt(coeff_grid)

    def vertical(upward, press):
        stacked = jnp.stack([upward, press], 0).reshape(2, levels, 16, length)
        columns = lax.all_to_all(stacked, "lev", split_axis=2, concat_axis=1, tiled=True)
        solved, press_new = column_step(columns[0], columns[1], coeff_grid, root_grid, 0)
        back = lax.all_to_all(
            jnp.stack([solved, press_new], 0), "lev", split_axis=1, concat_axis=2, tiled=True
        )
        back = back.reshape(2, levels, 4, 4, length)
        return (back[0], back[1])

    state = tuple((field.reshape(levels, 4, 4, length) for field in fields))
    for step in range(SUBSTEPS):
        state = substep(state, grid_mass, recip, "lijy", derivative, vertical)
    results = [field.reshape(levels, 16, length) for field in state]
    outputs = [jnp.take(field, order, axis=2) for field in results]
    return (outputs[0], outputs[1], outputs[2], outputs[3], outputs[4])


CHUNKS = 2
TILE = 8


def derivative_parts():
    points = np.array([-1.0, -1.0 / math.sqrt(5.0), 1.0 / math.sqrt(5.0), 1.0])
    matrix = np.zeros((4, 4))
    for a in range(4):
        for b in range(4):
            if a == b:
                matrix[a, b] = sum(1.0 / (points[a] - points[o]) for o in range(4) if o != a)
            else:
                top = math.prod(points[a] - points[o] for o in range(4) if o != a)
                low = math.prod(points[b] - points[o] for o in range(4) if o != b)
                matrix[a, b] = top / (low * (points[a] - points[b]))
    return matrix


MATRIX = derivative_parts()


def line(f0, f1, f2, f3, scale):
    outer, inner = f0 - f3, f1 - f2
    bend = (f0 + f3) - (f1 + f2)
    out = [None] * 4
    for a in (0, 1):
        m = MATRIX[a] * scale
        odd = float(0.5 * (m[0] - m[3])) * outer + float(0.5 * (m[1] - m[2])) * inner
        even = float(0.5 * (m[0] + m[3])) * bend
        out[a], out[3 - a] = odd + even, odd - even
    return out


def along_i(f, scale):
    out = [None] * 16
    for j in range(4):
        for i, value in enumerate(line(f[j], f[4 + j], f[8 + j], f[12 + j], scale)):
            out[4 * i + j] = value
    return out


def along_j(f, scale):
    out = [None] * 16
    for i in range(4):
        out[4 * i : 4 * i + 4] = line(*f[4 * i : 4 * i + 4], scale)
    return out


def ahead(x):
    return pltpu.roll(x, x.shape[1] - 1, 1)


def behind(x):
    return pltpu.roll(x, 1, 1)


def join_j(f):
    out = list(f)
    for i in range(4):
        shared = f[4 * i + 3] + ahead(f[4 * i])
        out[4 * i + 3] = shared
        out[4 * i] = behind(shared)
    return out


def lanes(x, index):
    return jnp.take_along_axis(x, index, axis=1, mode="promise_in_bounds")


def fused(
    strips,
    h_zon, h_mer, h_ver, h_pre, h_geo, h_lay, h_stf, inv_ref, ord_ref,
    o_zon, o_mer, o_ver, o_pre, o_geo,
    U, V, G, M, R, P, W, Z, C, I, H, A,
    s_m, r_m, s_uv, r_uv, s_w, r_w, s_d, r_d, s_g, r_g, s_e, r_e, r_a,
    zon, mer, ver, pre, geo, lay, stf, send_sem, recv_sem, load_sem,
):
    levels = U.shape[1]
    span = levels // CHUNKS
    tiles = span // TILE
    me = lax.axis_index("elem")
    lev = lax.axis_index("lev")
    left, right = lax.rem(me + strips - 1, strips), lax.rem(me + 1, strips)
    other = 1 - lev
    inv = inv_ref[...]
    order = ord_ref[...]
    quad = [1.0 / 6.0, 5.0 / 6.0, 5.0 / 6.0, 1.0 / 6.0]
    weights = [quad[n // 4] * quad[n % 4] for n in range(16)]
    started = []
    MESH = pl.DeviceIdType.MESH

    def send(src, dst, target):
        slot = len(started)
        copy = pltpu.make_async_remote_copy(
            src_ref=src, dst_ref=dst, send_sem=send_sem.at[slot], recv_sem=recv_sem.at[slot],
            device_id=target, device_id_type=MESH,
        )
        copy.start()
        started.append(copy)
        return copy

    def send_faces(out, back, step, c):
        return [
            send(out.at[step, 0, c], back.at[step, 0, c], {"elem": left}),
            send(out.at[step, 1, c], back.at[step, 1, c], {"elem": right}),
        ]

    def arrive(copies):
        for copy in copies:
            copy.wait_recv()

    def column_rows(n, l0):
        return (pl.ds(l0 * 16 + n, TILE, stride=16), slice(None))

    def node_rows(n, l0):
        return (n, pl.ds(l0, TILE), slice(None))

    def each_tile(c, work):
        def go(b, carry):
            work(pl.multiple_of(c * span + b * TILE, TILE), pl.multiple_of(b * TILE, TILE))
            return carry

        lax.fori_loop(0, tiles, go, 0)

    def put_faces(buf, step, c, at, b0, f):
        for j in range(3):
            buf[step, 0, c, at + j, pl.ds(b0, TILE), :] = f[j]
            buf[step, 1, c, at + j, pl.ds(b0, TILE), :] = f[12 + j]

    def total_faces(out, back, step, c, at, b0):
        result = {}
        for i, own, theirs in ((0, 0, 1), (3, 1, 0)):
            for j in range(3):
                result[4 * i + j] = (
                    out[step, own, c, at + j, pl.ds(b0, TILE), :]
                    + back[step, theirs, c, at + j, pl.ds(b0, TILE), :]
                )
            result[4 * i + 3] = ahead(result[4 * i])
        return result

    def fetch(src, dst, slot):
        half = dst.shape[0] // 2
        copies = []
        for part in range(2):
            rows = pl.ds(part * half, half)
            copy = pltpu.make_async_copy(src.at[rows], dst.at[rows], load_sem.at[2 * slot + part])
            copy.start()
            copies.append(copy)
        return copies

    def loaded(copies):
        for copy in copies:
            copy.wait()

    lay_in, pre_in = fetch(h_lay, lay, 0), fetch(h_pre, pre, 1)
    ver_in, geo_in = fetch(h_ver, ver, 2), fetch(h_geo, geo, 3)
    zon_in, mer_in = fetch(h_zon, zon, 4), fetch(h_mer, mer, 5)
    own = pl.ds(pl.multiple_of(lev * levels, 8), levels)
    stf_in = pltpu.make_async_copy(h_stf.at[own], stf, load_sem.at[12])
    stf_in.start()

    barrier = pltpu.get_barrier_semaphore()
    for target in ({"elem": left}, {"elem": right}, {"lev": other}):
        pl.semaphore_signal(barrier, inc=1, device_id=target, device_id_type=MESH)
    pl.semaphore_wait(barrier, 3)

    stiff_copy = send(h_stf.at[pl.ds(pl.multiple_of(other * levels, 8), levels)], r_a, {"lev": other})

    def gather_rows(src, dst, c):
        def go(b, carry):
            for q in range(16):
                at = pl.ds(pl.multiple_of(c * span * 16 + b * 128 + q * 8, 8), 8)
                dst[at, :] = lanes(src[at, :], inv)
            return carry

        lax.fori_loop(0, tiles, go, 0)

    def load_mass(c):
        def work(l0, b0):
            m = [lanes(lay[column_rows(n, l0)], inv) * weights[n] for n in range(16)]
            for n in range(16):
                M[node_rows(n, l0)] = m[n]
            m = join_j(m)
            for n in range(4, 12):
                R[node_rows(n, l0)] = 1.0 / m[n]
            put_faces(s_m, 0, c, 0, b0, m)

        each_tile(c, work)

    def wind_step(step, c):
        def work(l0, b0):
            p = [P[column_rows(n, l0)] for n in range(16)]
            m = [M[node_rows(n, l0)] for n in range(16)]
            for at, field, d in ((0, U, along_i), (3, V, along_j)):
                t = join_j([x * y for x, y in zip(m, d(p, -horizontal_speed))])
                for n in range(4, 12):
                    add = R[node_rows(n, l0)] * t[n]
                    field[node_rows(n, l0)] = add if step == 0 else field[node_rows(n, l0)] + add
                put_faces(s_uv, step, c, at, b0, t)

        each_tile(c, work)

    def start_winds(c):
        def work(l0, b0):
            for src, field in ((zon, U), (mer, V)):
                for n in range(16):
                    value = lanes(src[column_rows(n, l0)], inv)
                    if 4 <= n < 12:
                        value = value + field[node_rows(n, l0)]
                    field[node_rows(n, l0)] = value

        each_tile(c, work)

    def drift(f, m):
        first, second = along_i(f, -drift_first), along_j(f, -drift_second)
        return join_j([k * (x + y) for k, x, y in zip(m, first, second)])

    def vertical_step(step, c):
        def work(l0, b0):
            m = [M[node_rows(n, l0)] for n in range(16)]
            w = [W[column_rows(n, l0)] for n in range(16)]
            for n in range(16):
                if step == 0:
                    G[node_rows(n, l0)] = lanes(geo[column_rows(n, l0)], inv)
                else:
                    G[node_rows(n, l0)] = G[node_rows(n, l0)] + geopotential_rate * w[n]
            t = drift(w, m)
            for n in range(4, 12):
                W[column_rows(n, l0)] = w[n] + R[node_rows(n, l0)] * t[n]
            put_faces(s_w, step, c, 0, b0, t)

        each_tile(c, work)

    def geopotential_step(step, c):
        def work(l0, b0):
            m = [M[node_rows(n, l0)] for n in range(16)]
            g = [G[node_rows(n, l0)] for n in range(16)]
            t = drift(g, m)
            for n in range(4, 12):
                G[node_rows(n, l0)] = g[n] + R[node_rows(n, l0)] * t[n]
            put_faces(s_g, step, c, 0, b0, t)

        each_tile(c, work)

    def mass_faces(c):
        def work(l0, b0):
            for n, total in total_faces(s_m, r_m, 0, c, 0, b0).items():
                R[node_rows(n, l0)] = 1.0 / total

        each_tile(c, work)

    def divergence_step(step, c):
        def work(l0, b0):
            for at, field in ((0, U), (3, V)):
                for n, total in total_faces(s_uv, r_uv, step, c, at, b0).items():
                    field[node_rows(n, l0)] = field[node_rows(n, l0)] + R[node_rows(n, l0)] * total
            m = [M[node_rows(n, l0)] for n in range(16)]
            du = along_i([U[node_rows(n, l0)] for n in range(16)], -horizontal_speed)
            dv = along_j([V[node_rows(n, l0)] for n in range(16)], -horizontal_speed)
            t = join_j([k * (x + y) for k, x, y in zip(m, du, dv)])
            for n in range(4, 12):
                P[column_rows(n, l0)] = P[column_rows(n, l0)] + R[node_rows(n, l0)] * t[n]
            put_faces(s_d, step, c, 0, b0, t)

        each_tile(c, work)

    def column_faces(field, out, back, step, c):
        def work(l0, b0):
            for n, total in total_faces(out, back, step, c, 0, b0).items():
                field[column_rows(n, l0)] = field[column_rows(n, l0)] + R[node_rows(n, l0)] * total

        each_tile(c, work)

    def geopotential_faces(step, c):
        def work(l0, b0):
            for n, total in total_faces(s_g, r_g, step, c, 0, b0).items():
                G[node_rows(n, l0)] = G[node_rows(n, l0)] + R[node_rows(n, l0)] * total

        each_tile(c, work)

    def row(e):
        k = e + lev * (levels - 1 - 2 * e)
        return pl.ds(pl.multiple_of(k * 16, 16), 16)

    side = (1 - 2 * lev).astype(jnp.float32)
    zero = jnp.zeros((16, P.shape[1]), jnp.float32)

    def factor():
        def fill(k, carry):
            mine = lanes(stf[k], inv)
            theirs = lanes(r_a[k], inv)
            top = jnp.where(lev == 0, mine, theirs)
            bottom = jnp.where(lev == 0, theirs, mine)
            both = jnp.concatenate([top, bottom], 0)
            at = pl.ds(pl.multiple_of(k * 16, 16), 16)
            A[at, :] = both
            H[at, :] = jnp.sqrt(both) * (0.5 * side)
            return carry

        lax.fori_loop(0, levels, fill, 0, unroll=4)

        def go(block, ratio):
            for u in range(4):
                at = row(block * 4 + u)
                a = A[at, :]
                turn = 1.0 / (1.0 + 2.0 * a - a * ratio)
                ratio = a * turn
                C[at, :] = ratio
                I[at, :] = turn
            return ratio

        lax.fori_loop(0, levels // 4, go, zero)
        at = row(levels - 1)
        s_e[0, 0] = C[at, :]
        s_e[0, 1] = H[at, :] * I[at, :]
        return send(s_e.at[0], r_e.at[0], {"lev": other})

    def eliminate(step):
        def one(e, before, here, after, z):
            at = row(e)
            z = (W[at, :] - H[at, :] * (after - before)) * I[at, :] + C[at, :] * z
            Z[at, :] = z
            return here, after, z

        def go(block, carry):
            before, here, z = carry
            for u in range(8):
                e = block * 8 + u
                after = P[row(e + 1), :]
                before, here, z = one(e, before, here, after, z)
            return before, here, z

        carry = lax.fori_loop(0, levels // 8 - 1, go, (zero, P[row(0), :], zero))
        before, here, z = carry
        for u in range(8):
            e = levels - 8 + u
            after = P[row(e + 1), :] if u < 7 else zero
            before, here, z = one(e, before, here, after, z)
        s_e[step + 1, 0] = z
        s_e[step + 1, 1] = before
        return send(s_e.at[step + 1], r_e.at[step + 1], {"lev": other})

    def substitute(step):
        ratio, pull = s_e[0, 0], s_e[0, 1]
        ratio_other, pull_other = r_e[0, 0], r_e[0, 1]
        z = s_e[step + 1, 0] - pull * r_e[step + 1, 1]
        z_other = r_e[step + 1, 0] - pull_other * s_e[step + 1, 1]
        x = (z + ratio * z_other) / (1.0 - ratio * ratio_other)
        beyond = z_other + ratio_other * x
        W[row(levels - 1), :] = x

        def one(e, beyond, x):
            here = Z[row(e), :] + C[row(e), :] * x
            W[row(e), :] = here
            at = row(e + 1)
            P[at, :] = P[at, :] - H[at, :] * (beyond - here)
            return x, here

        carry = (beyond, x)
        for u in range(7):
            carry = one(levels - 2 - u, *carry)

        def go(block, carry):
            for u in range(8):
                carry = one(levels - 9 - block * 8 - u, *carry)
            return carry

        beyond, x = lax.fori_loop(0, levels // 8 - 1, go, carry)
        at = row(0)
        P[at, :] = P[at, :] - H[at, :] * beyond

    def write_nodes(field, out, c):
        def work(l0, b0):
            for n in range(16):
                out[column_rows(n, l0)] = lanes(field[node_rows(n, l0)], order)

        each_tile(c, work)

    def write_geopotential(c):
        def work(l0, b0):
            for n in range(16):
                value = G[node_rows(n, l0)] + geopotential_rate * W[column_rows(n, l0)]
                o_geo[column_rows(n, l0)] = lanes(value, order)

        each_tile(c, work)

    def write_rows(field, out):
        def go(b, carry):
            for q in range(16):
                at = pl.ds(pl.multiple_of(b * 128 + q * 8, 8), 8)
                out[at, :] = lanes(field[at, :], order)
            return carry

        lax.fori_loop(0, levels // TILE, go, 0)

    edge_copy = None
    for step in range(SUBSTEPS):
        uv, w, d, g, m = [], [], [], [], []
        for c in range(CHUNKS):
            if step == 0:
                if c == 0:
                    loaded(lay_in)
                load_mass(c)
                m.append(send_faces(s_m, r_m, 0, c))
                if c == 0:
                    loaded(pre_in)
                gather_rows(pre, P, c)
            wind_step(step, c)
            uv.append(send_faces(s_uv, r_uv, step, c))
        for c in range(CHUNKS):
            if step == 0:
                if c == 0:
                    loaded(ver_in + geo_in)
                gather_rows(ver, W, c)
            vertical_step(step, c)
            w.append(send_faces(s_w, r_w, step, c))
        if step == 0:
            loaded(zon_in + mer_in)
            for c in range(CHUNKS):
                start_winds(c)
                arrive(m[c])
                mass_faces(c)
        for c in range(CHUNKS):
            arrive(uv[c])
            divergence_step(step, c)
            d.append(send_faces(s_d, r_d, step, c))
        for c in range(CHUNKS):
            geopotential_step(step, c)
            g.append(send_faces(s_g, r_g, step, c))
        if step == 0:
            stf_in.wait()
            stiff_copy.wait_recv()
            edge_copy = factor()
        if step == SUBSTEPS - 1:
            for c in range(CHUNKS):
                write_nodes(U, o_zon, c)
                write_nodes(V, o_mer, c)
        for c in range(CHUNKS):
            arrive(w[c])
            column_faces(W, s_w, r_w, step, c)
        for c in range(CHUNKS):
            arrive(d[c])
            column_faces(P, s_d, r_d, step, c)
        message = eliminate(step)
        for c in range(CHUNKS):
            arrive(g[c])
            geopotential_faces(step, c)
        if step == 0:
            edge_copy.wait_recv()
        message.wait_recv()
        substitute(step)
    for c in range(CHUNKS):
        write_geopotential(c)
    write_rows(W, o_ver)
    write_rows(P, o_pre)
    for copy in started:
        copy.wait_send()


def store(a, b, c, d, e, p, q, r, s, t, sem):
    copies = []
    for src, dst in ((a, p), (b, q), (c, r), (d, s), (e, t)):
        half = src.shape[0] // 2
        for part in range(2):
            rows = pl.ds(part * half, half)
            copy = pltpu.make_async_copy(src.at[rows], dst.at[rows], sem.at[len(copies)])
            copy.start()
            copies.append(copy)
    for copy in copies:
        copy.wait()


def pair_step(
    strips, zonal_wind, meridional_wind, vertical_wind, pressure, geopotential, layer_mass,
    stiffness, elem_order,
):
    levels, nodes, length = zonal_wind.shape
    order = elem_order[0]
    slots = jnp.arange(length, dtype=jnp.int32)
    inverse = jnp.sum(jnp.where(order[:, None] == slots[None, :], slots[:, None], 0), axis=0)
    inv = jnp.broadcast_to(inverse[None, :], (TILE, length))
    back = jnp.broadcast_to(elem_order, (TILE, length))
    fields = [
        f.reshape(levels * nodes, length)
        for f in (zonal_wind, meridional_wind, vertical_wind, pressure, geopotential, layer_mass)
    ]
    span = levels // CHUNKS

    def faces(steps, count):
        return [pltpu.VMEM((steps, 2, CHUNKS, count, span, length), jnp.float32)] * 2

    node_major = pltpu.VMEM((nodes, levels, length), jnp.float32)
    level_major = pltpu.VMEM((levels * nodes, length), jnp.float32)
    edges = pltpu.VMEM((SUBSTEPS + 1, 2, nodes, length), jnp.float32)
    copies = 1 + 2 * CHUNKS + SUBSTEPS * 8 * CHUNKS + 1 + SUBSTEPS
    vmem = pl.BlockSpec(memory_space=pltpu.VMEM)
    outputs = pl.pallas_call(
        functools.partial(fused, strips),
        out_shape=[pltpu.VMEM((levels * nodes, length), jnp.float32)] * 5,
        in_specs=[pl.BlockSpec(memory_space=pltpu.HBM)] * 7 + [vmem] * 2,
        out_specs=[vmem] * 5,
        scratch_shapes=[node_major] * 5
        + [level_major] * 7
        + faces(1, 3)
        + faces(SUBSTEPS, 6)
        + faces(SUBSTEPS, 3)
        + faces(SUBSTEPS, 3)
        + faces(SUBSTEPS, 3)
        + [edges, edges, pltpu.VMEM((levels, nodes // 2, length), jnp.float32)]
        + [level_major] * 6
        + [pltpu.VMEM((levels, nodes // 2, length), jnp.float32)]
        + [pltpu.SemaphoreType.DMA((copies,)), pltpu.SemaphoreType.DMA((copies,))]
        + [pltpu.SemaphoreType.DMA((13,))],
        compiler_params=pltpu.CompilerParams(
            collective_id=0, has_side_effects=True, vmem_limit_bytes=52 * 1024 * 1024
        ),
        name="acoustic_substeps",
    )(*fields, stiffness, inv, back)
    outputs = pl.pallas_call(
        store,
        out_shape=[jax.ShapeDtypeStruct((levels * nodes, length), jnp.float32)] * 5,
        in_specs=[vmem] * 5,
        out_specs=[pl.BlockSpec(memory_space=pl.ANY)] * 5,
        scratch_shapes=[pltpu.SemaphoreType.DMA((10,))],
        name="store_outputs",
    )(*outputs)
    return tuple(f.reshape(levels, nodes, length) for f in outputs)


def local_step(strips, pair, *arrays):
    levels, nodes, length = arrays[0].shape
    if pair == 2 and strips > 2 and nodes == 16 and length == 128 and levels % (CHUNKS * TILE) == 0:
        return pair_step(strips, *arrays)
    return body(*arrays)


def solution(mesh):
    placed = (
        P("lev", None, "elem"),
        P("lev", None, "elem"),
        P("lev", None, "elem"),
        P("lev", None, "elem"),
        P("lev", None, "elem"),
        P("lev", None, "elem"),
        P(None, "lev", "elem"),
        P("elem", None),
    )
    return jax.shard_map(
        functools.partial(local_step, mesh.shape["elem"], mesh.shape["lev"]),
        mesh=mesh,
        in_specs=placed,
        out_specs=(
            P("lev", None, "elem"),
            P("lev", None, "elem"),
            P("lev", None, "elem"),
            P("lev", None, "elem"),
            P("lev", None, "elem"),
        ),
        check_vma=False,
    )
```

```python
import functools
import math

import jax
import jax.numpy as jnp
import numpy as np
from jax import lax
from jax.experimental import pallas as pl
from jax.experimental.pallas import tpu as pltpu
from jax.sharding import PartitionSpec as P

SUBSTEPS = 3


horizontal_speed = 0.12
drift_first = 0.1
drift_second = 0.06
geopotential_rate = 2.0


def padded(cells, sides, width):
    for axis, dim in sides:
        count = lax.axis_size(axis)
        head = lax.slice_in_dim(cells, 0, width, axis=dim)
        tail = lax.slice_in_dim(cells, cells.shape[dim] - width, cells.shape[dim], axis=dim)
        cells = jnp.concatenate(
            [
                lax.ppermute(tail, axis, [(i, (i + 1) % count) for i in range(count)]),
                cells,
                lax.ppermute(head, axis, [((i + 1) % count, i) for i in range(count)]),
            ],
            axis=dim,
        )
    return cells


def gll_tables():
    points = np.array([-1.0, -1.0 / math.sqrt(5.0), 1.0 / math.sqrt(5.0), 1.0])
    quadrature = np.array([1.0 / 6.0, 5.0 / 6.0, 5.0 / 6.0, 1.0 / 6.0])
    derivative = np.zeros((4, 4))
    for target in range(4):
        for source in range(4):
            if target == source:
                derivative[target, source] = sum(
                    (
                        1.0 / (points[target] - points[other])
                        for other in range(4)
                        if other != target
                    )
                )
            else:
                top_term = math.prod(
                    (points[target] - points[other] for other in range(4) if other != target)
                )
                low_term = math.prod(
                    (points[source] - points[other] for other in range(4) if other != source)
                )
                derivative[target, source] = top_term / (
                    low_term * (points[target] - points[source])
                )
    return (
        jnp.asarray(derivative, jnp.float32),
        jnp.asarray(np.outer(quadrature, quadrature).reshape(16), jnp.float32),
    )


def derivative_along(field, letters, which, derivative):
    result = letters.replace(which, "a")
    return jnp.einsum(
        "a" + which + "," + letters + "->" + result,
        derivative,
        field,
        precision=lax.Precision.HIGHEST,
    )


def assemble(stacked):
    axis_i, axis_j, axis_y = (2, 3, 4)
    left = lax.index_in_dim(stacked, 0, axis_i, keepdims=False)
    right = lax.index_in_dim(stacked, 3, axis_i, keepdims=False)
    faces = jnp.stack([left, right], 0)
    extended = padded(faces, (("elem", 0),), 1)
    left = left + extended[0]
    right = right + extended[3]
    stacked = jnp.concatenate(
        [
            jnp.expand_dims(left, axis_i),
            lax.slice_in_dim(stacked, 1, 3, axis=axis_i),
            jnp.expand_dims(right, axis_i),
        ],
        axis_i,
    )
    lower = lax.index_in_dim(stacked, 0, axis_j, keepdims=False)
    upper = lax.index_in_dim(stacked, 3, axis_j, keepdims=False)
    faces = jnp.stack([lower, upper], 0)
    length = faces.shape[axis_y]
    extended = jnp.concatenate(
        [
            lax.slice_in_dim(faces, length - 1, length, axis=axis_y),
            faces,
            lax.slice_in_dim(faces, 0, 1, axis=axis_y),
        ],
        axis_y,
    )
    lower = lower + lax.slice_in_dim(extended[1], 0, length, axis=axis_y - 1)
    upper = upper + lax.slice_in_dim(extended[0], 2, length + 2, axis=axis_y - 1)
    return jnp.concatenate(
        [
            jnp.expand_dims(lower, axis_j),
            lax.slice_in_dim(stacked, 1, 3, axis=axis_j),
            jnp.expand_dims(upper, axis_j),
        ],
        axis_j,
    )


def lift(field, stride, axis, fill):
    length = field.shape[axis]
    kept = lax.slice_in_dim(field, stride, length, axis=axis)
    padding = jnp.full_like(lax.slice_in_dim(field, 0, stride, axis=axis), fill)
    return jnp.concatenate([kept, padding], axis)


def sink(field, stride, axis, fill):
    length = field.shape[axis]
    kept = lax.slice_in_dim(field, 0, length - stride, axis=axis)
    padding = jnp.full_like(lax.slice_in_dim(field, 0, stride, axis=axis), fill)
    return jnp.concatenate([padding, kept], axis)


def column_step(upward, press, coeff, root, axis):
    rhs = upward - root * 0.5 * (lift(press, 1, axis, 0.0) - sink(press, 1, axis, 0.0))
    lower = -coeff
    upper = -coeff
    middle = 1.0 + 2.0 * coeff
    length = coeff.shape[axis]
    stride = 1
    while stride < length:
        from_below = -lower / sink(middle, stride, axis, 1.0)
        from_above = -upper / lift(middle, stride, axis, 1.0)
        new_lower = from_below * sink(lower, stride, axis, 0.0)
        new_upper = from_above * lift(upper, stride, axis, 0.0)
        middle = (
            middle
            + from_below * sink(upper, stride, axis, 0.0)
            + from_above * lift(lower, stride, axis, 0.0)
        )
        rhs = (
            rhs
            + from_below * sink(rhs, stride, axis, 0.0)
            + from_above * lift(rhs, stride, axis, 0.0)
        )
        lower, upper = (new_lower, new_upper)
        stride = stride * 2
    solved = rhs / middle
    press = press - root * 0.5 * (lift(solved, 1, axis, 0.0) - sink(solved, 1, axis, 0.0))
    return (solved, press)


def substep(state, mass, recip, letters, derivative, vertical):
    zonal, meridional, upward, press, geopot = state
    tendencies = jnp.stack(
        [
            mass * (-horizontal_speed * derivative_along(press, letters, "i", derivative)),
            mass * (-horizontal_speed * derivative_along(press, letters, "j", derivative)),
            mass
            * -(
                drift_first * derivative_along(upward, letters, "i", derivative)
                + drift_second * derivative_along(upward, letters, "j", derivative)
            ),
            mass
            * -(
                drift_first * derivative_along(geopot, letters, "i", derivative)
                + drift_second * derivative_along(geopot, letters, "j", derivative)
            ),
        ],
        0,
    )
    summed = assemble(tendencies)
    zonal = zonal + recip * summed[0]
    meridional = meridional + recip * summed[1]
    upward = upward + recip * summed[2]
    geopot = geopot + recip * summed[3]
    divergence = derivative_along(zonal, letters, "i", derivative) + derivative_along(
        meridional, letters, "j", derivative
    )
    press = press + recip * assemble(jnp.expand_dims(mass * (-horizontal_speed * divergence), 0))[0]
    solved, press = vertical(upward, press)
    geopot = geopot + geopotential_rate * solved
    return (zonal, meridional, solved, press, geopot)


def body(
    zonal_wind,
    meridional_wind,
    vertical_wind,
    pressure,
    geopotential,
    layer_mass,
    stiffness,
    elem_order,
):
    derivative, weights = gll_tables()
    order = elem_order[0]
    length = order.shape[0]
    inverse = jnp.zeros((length,), jnp.int32).at[order].set(jnp.arange(length, dtype=jnp.int32))
    levels = zonal_wind.shape[0]
    fields = [
        jnp.take(field, inverse, axis=2)
        for field in (zonal_wind, meridional_wind, vertical_wind, pressure, geopotential)
    ]
    mass = jnp.take(layer_mass, inverse, axis=2) * weights[None, :, None]
    coeff_grid = jnp.take(stiffness, inverse, axis=2)
    grid_mass = mass.reshape(levels, 4, 4, length)
    recip = 1.0 / assemble(jnp.expand_dims(grid_mass, 0))[0]
    root_grid = jnp.sqrt(coeff_grid)

    def vertical(upward, press):
        stacked = jnp.stack([upward, press], 0).reshape(2, levels, 16, length)
        columns = lax.all_to_all(stacked, "lev", split_axis=2, concat_axis=1, tiled=True)
        solved, press_new = column_step(columns[0], columns[1], coeff_grid, root_grid, 0)
        back = lax.all_to_all(
            jnp.stack([solved, press_new], 0), "lev", split_axis=1, concat_axis=2, tiled=True
        )
        back = back.reshape(2, levels, 4, 4, length)
        return (back[0], back[1])

    state = tuple((field.reshape(levels, 4, 4, length) for field in fields))
    for step in range(SUBSTEPS):
        state = substep(state, grid_mass, recip, "lijy", derivative, vertical)
    results = [field.reshape(levels, 16, length) for field in state]
    outputs = [jnp.take(field, order, axis=2) for field in results]
    return (outputs[0], outputs[1], outputs[2], outputs[3], outputs[4])


CHUNKS = 4
TILE = 8


def derivative_parts():
    points = np.array([-1.0, -1.0 / math.sqrt(5.0), 1.0 / math.sqrt(5.0), 1.0])
    matrix = np.zeros((4, 4))
    for a in range(4):
        for b in range(4):
            if a == b:
                matrix[a, b] = sum(1.0 / (points[a] - points[o]) for o in range(4) if o != a)
            else:
                top = math.prod(points[a] - points[o] for o in range(4) if o != a)
                low = math.prod(points[b] - points[o] for o in range(4) if o != b)
                matrix[a, b] = top / (low * (points[a] - points[b]))
    return matrix


MATRIX = derivative_parts()


def line(f0, f1, f2, f3, scale):
    outer, inner = f0 - f3, f1 - f2
    bend = (f0 + f3) - (f1 + f2)
    out = [None] * 4
    for a in (0, 1):
        m = MATRIX[a] * scale
        odd = float(0.5 * (m[0] - m[3])) * outer + float(0.5 * (m[1] - m[2])) * inner
        even = float(0.5 * (m[0] + m[3])) * bend
        out[a], out[3 - a] = odd + even, odd - even
    return out


def along_i(f, scale):
    out = [None] * 16
    for j in range(4):
        for i, value in enumerate(line(f[j], f[4 + j], f[8 + j], f[12 + j], scale)):
            out[4 * i + j] = value
    return out


def along_j(f, scale):
    out = [None] * 16
    for i in range(4):
        out[4 * i : 4 * i + 4] = line(*f[4 * i : 4 * i + 4], scale)
    return out


def ahead(x):
    return pltpu.roll(x, x.shape[1] - 1, 1)


def behind(x):
    return pltpu.roll(x, 1, 1)


def join_j(f):
    out = list(f)
    for i in range(4):
        shared = f[4 * i + 3] + ahead(f[4 * i])
        out[4 * i + 3] = shared
        out[4 * i] = behind(shared)
    return out


def lanes(x, index):
    return jnp.take_along_axis(x, index, axis=1, mode="promise_in_bounds")


def fused(
    strips,
    h_zon, h_mer, h_ver, h_pre, h_geo, h_lay, h_stf, h_ord,
    q_zon, q_mer, q_ver, q_pre, q_geo,
    U, V, G, M, R, P, W, Z, C, I, H, A,
    s_m, r_m, s_uv, r_uv, s_w, r_w, s_d, r_d, s_g, r_g, s_e, r_e, r_a,
    zon, mer, ver, pre, geo, lay, stf, ord_ref,
    o_zon, o_mer, o_ver, o_pre, o_geo, send_sem, recv_sem, load_sem, store_sem,
):
    levels = U.shape[1]
    span = levels // CHUNKS
    tiles = span // TILE
    me = lax.axis_index("elem")
    lev = lax.axis_index("lev")
    left, right = lax.rem(me + strips - 1, strips), lax.rem(me + 1, strips)
    other = 1 - lev
    sequence = [c + lev * (CHUNKS - 1 - 2 * c) for c in range(CHUNKS)]
    quad = [1.0 / 6.0, 5.0 / 6.0, 5.0 / 6.0, 1.0 / 6.0]
    weights = [quad[n // 4] * quad[n % 4] for n in range(16)]
    started = []
    MESH = pl.DeviceIdType.MESH

    def send(src, dst, target):
        slot = len(started)
        copy = pltpu.make_async_remote_copy(
            src_ref=src, dst_ref=dst, send_sem=send_sem.at[slot], recv_sem=recv_sem.at[slot],
            device_id=target, device_id_type=MESH,
        )
        copy.start()
        started.append(copy)
        return copy

    def send_faces(out, back, step, c):
        return [
            send(out.at[step, 0, c], back.at[step, 0, c], {"elem": left}),
            send(out.at[step, 1, c], back.at[step, 1, c], {"elem": right}),
        ]

    def arrive(copies):
        for copy in copies:
            copy.wait_recv()

    def column_rows(n, l0):
        return (pl.ds(l0 * 16 + n, TILE, stride=16), slice(None))

    def node_rows(n, l0):
        return (n, pl.ds(l0, TILE), slice(None))

    def each_tile(c, work):
        def go(b, carry):
            work(pl.multiple_of(c * span + b * TILE, TILE), pl.multiple_of(b * TILE, TILE))
            return carry

        lax.fori_loop(0, tiles, go, 0)

    def put_faces(buf, step, c, at, b0, f):
        for j in range(3):
            buf[step, 0, c, at + j, pl.ds(b0, TILE), :] = f[j]
            buf[step, 1, c, at + j, pl.ds(b0, TILE), :] = f[12 + j]

    def total_faces(out, back, step, c, at, b0):
        result = {}
        for i, own, theirs in ((0, 0, 1), (3, 1, 0)):
            for j in range(3):
                result[4 * i + j] = (
                    out[step, own, c, at + j, pl.ds(b0, TILE), :]
                    + back[step, theirs, c, at + j, pl.ds(b0, TILE), :]
                )
            result[4 * i + 3] = ahead(result[4 * i])
        return result

    def fetch(src, dst, slot):
        half = dst.shape[0] // 2
        copies = []
        for part in range(2):
            rows = pl.ds(part * half, half)
            copy = pltpu.make_async_copy(src.at[rows], dst.at[rows], load_sem.at[2 * slot + part])
            copy.start()
            copies.append(copy)
        return copies

    def loaded(copies):
        for copy in copies:
            copy.wait()

    order_in = pltpu.make_async_copy(h_ord, ord_ref, load_sem.at[13])
    order_in.start()
    lay_in, pre_in = fetch(h_lay, lay, 0), fetch(h_pre, pre, 1)
    ver_in, geo_in = fetch(h_ver, ver, 2), fetch(h_geo, geo, 3)
    zon_in, mer_in = fetch(h_zon, zon, 4), fetch(h_mer, mer, 5)
    own = pl.ds(pl.multiple_of(lev * levels, 8), levels)
    stf_in = pltpu.make_async_copy(h_stf.at[own], stf, load_sem.at[12])
    stf_in.start()

    barrier = pltpu.get_barrier_semaphore()
    for target in ({"elem": left}, {"elem": right}, {"lev": other}):
        pl.semaphore_signal(barrier, inc=1, device_id=target, device_id_type=MESH)
    pl.semaphore_wait(barrier, 3)

    stiff_copy = send(h_stf.at[pl.ds(pl.multiple_of(other * levels, 8), levels)], r_a, {"lev": other})

    order_in.wait()
    order = jnp.broadcast_to(ord_ref[...], (TILE, ord_ref.shape[1]))
    lane = lax.broadcasted_iota(jnp.int32, order.shape, 1)
    inv = jnp.zeros_like(order)
    for turn in range(order.shape[1]):
        moved = pltpu.roll(order, turn, 1) if turn else order
        source = jnp.where(lane >= turn, lane - turn, lane - turn + order.shape[1])
        inv = jnp.where(moved == lane, source, inv)

    def gather_rows(src, dst, c):
        def go(b, carry):
            for q in range(16):
                at = pl.ds(pl.multiple_of(c * span * 16 + b * 128 + q * 8, 8), 8)
                dst[at, :] = lanes(src[at, :], inv)
            return carry

        lax.fori_loop(0, tiles, go, 0)

    def load_mass(c):
        def work(l0, b0):
            m = [lanes(lay[column_rows(n, l0)], inv) * weights[n] for n in range(16)]
            for n in range(16):
                M[node_rows(n, l0)] = m[n]
            m = join_j(m)
            for n in range(4, 12):
                R[node_rows(n, l0)] = 1.0 / m[n]
            put_faces(s_m, 0, c, 0, b0, m)

        each_tile(c, work)

    def wind_step(step, c):
        def work(l0, b0):
            p = [P[column_rows(n, l0)] for n in range(16)]
            m = [M[node_rows(n, l0)] for n in range(16)]
            for at, field, d in ((0, U, along_i), (3, V, along_j)):
                t = join_j([x * y for x, y in zip(m, d(p, -horizontal_speed))])
                for n in range(4, 12):
                    add = R[node_rows(n, l0)] * t[n]
                    field[node_rows(n, l0)] = add if step == 0 else field[node_rows(n, l0)] + add
                put_faces(s_uv, step, c, at, b0, t)

        each_tile(c, work)

    def start_winds(c):
        def work(l0, b0):
            for src, field in ((zon, U), (mer, V)):
                for n in range(16):
                    value = lanes(src[column_rows(n, l0)], inv)
                    if 4 <= n < 12:
                        value = value + field[node_rows(n, l0)]
                    field[node_rows(n, l0)] = value

        each_tile(c, work)

    def drift(f, m):
        first, second = along_i(f, -drift_first), along_j(f, -drift_second)
        return join_j([k * (x + y) for k, x, y in zip(m, first, second)])

    def vertical_step(step, c):
        def work(l0, b0):
            m = [M[node_rows(n, l0)] for n in range(16)]
            w = [W[column_rows(n, l0)] for n in range(16)]
            for n in range(16):
                if step == 0:
                    G[node_rows(n, l0)] = lanes(geo[column_rows(n, l0)], inv)
                else:
                    G[node_rows(n, l0)] = G[node_rows(n, l0)] + geopotential_rate * w[n]
            t = drift(w, m)
            for n in range(4, 12):
                W[column_rows(n, l0)] = w[n] + R[node_rows(n, l0)] * t[n]
            put_faces(s_w, step, c, 0, b0, t)

        each_tile(c, work)

    def geopotential_step(step, c):
        def work(l0, b0):
            m = [M[node_rows(n, l0)] for n in range(16)]
            g = [G[node_rows(n, l0)] for n in range(16)]
            t = drift(g, m)
            for n in range(4, 12):
                G[node_rows(n, l0)] = g[n] + R[node_rows(n, l0)] * t[n]
            put_faces(s_g, step, c, 0, b0, t)

        each_tile(c, work)

    def mass_faces(c):
        def work(l0, b0):
            for n, total in total_faces(s_m, r_m, 0, c, 0, b0).items():
                R[node_rows(n, l0)] = 1.0 / total

        each_tile(c, work)

    def divergence_step(step, c):
        def work(l0, b0):
            for at, field in ((0, U), (3, V)):
                for n, total in total_faces(s_uv, r_uv, step, c, at, b0).items():
                    field[node_rows(n, l0)] = field[node_rows(n, l0)] + R[node_rows(n, l0)] * total
            m = [M[node_rows(n, l0)] for n in range(16)]
            du = along_i([U[node_rows(n, l0)] for n in range(16)], -horizontal_speed)
            dv = along_j([V[node_rows(n, l0)] for n in range(16)], -horizontal_speed)
            t = join_j([k * (x + y) for k, x, y in zip(m, du, dv)])
            for n in range(4, 12):
                P[column_rows(n, l0)] = P[column_rows(n, l0)] + R[node_rows(n, l0)] * t[n]
            put_faces(s_d, step, c, 0, b0, t)

        each_tile(c, work)

    def column_faces(field, out, back, step, c):
        def work(l0, b0):
            for n, total in total_faces(out, back, step, c, 0, b0).items():
                field[column_rows(n, l0)] = field[column_rows(n, l0)] + R[node_rows(n, l0)] * total

        each_tile(c, work)

    def geopotential_faces(step, c):
        def work(l0, b0):
            for n, total in total_faces(s_g, r_g, step, c, 0, b0).items():
                G[node_rows(n, l0)] = G[node_rows(n, l0)] + R[node_rows(n, l0)] * total

        each_tile(c, work)

    stride = 16 - 32 * lev
    outer = lev * ((levels - 1) * 16)

    def row(e):
        return pl.ds(pl.multiple_of(outer + stride * e, 16), 16)

    side = (1 - 2 * lev).astype(jnp.float32)
    zero = jnp.zeros((16, P.shape[1]), jnp.float32)

    def factor():
        def fill(k, carry):
            mine = lanes(stf[k], inv)
            theirs = lanes(r_a[k], inv)
            top = jnp.where(lev == 0, mine, theirs)
            bottom = jnp.where(lev == 0, theirs, mine)
            both = jnp.concatenate([top, bottom], 0)
            at = pl.ds(pl.multiple_of(k * 16, 16), 16)
            A[at, :] = both
            H[at, :] = jnp.sqrt(both) * (0.5 * side)
            return carry

        lax.fori_loop(0, levels, fill, 0, unroll=4)

        def go(block, ratio):
            for u in range(4):
                at = row(block * 4 + u)
                a = A[at, :]
                turn = 1.0 / (1.0 + 2.0 * a - a * ratio)
                ratio = a * turn
                C[at, :] = ratio
                I[at, :] = turn
            return ratio

        lax.fori_loop(0, levels // 4, go, zero)
        at = row(levels - 1)
        s_e[0, 0] = C[at, :]
        s_e[0, 1] = H[at, :] * I[at, :]
        return send(s_e.at[0], r_e.at[0], {"lev": other})

    def eliminate(step, c, carry):
        def one(e, before, here, after, z):
            at = row(e)
            z = (W[at, :] - H[at, :] * (after - before)) * I[at, :] + C[at, :] * z
            Z[at, :] = z
            return here, after, z

        def block(b, carry):
            before, here, z = carry
            for u in range(8):
                e = c * span + b * 8 + u - 1
                before, here, z = one(e, before, here, P[row(e + 1), :], z)
            return before, here, z

        if c == 0:
            before, here, z = zero, P[row(0), :], zero
            for u in range(7):
                before, here, z = one(u, before, here, P[row(u + 1), :], z)
            carry = (before, here, z)
        carry = lax.fori_loop(1 if c == 0 else 0, tiles, block, carry)
        if c < CHUNKS - 1:
            return carry
        before, here, z = carry
        last, _, z = one(levels - 1, before, here, zero, z)
        s_e[step + 1, 0] = z
        s_e[step + 1, 1] = last
        return send(s_e.at[step + 1], r_e.at[step + 1], {"lev": other})

    def interface(step):
        ratio, pull = s_e[0, 0], s_e[0, 1]
        ratio_other, pull_other = r_e[0, 0], r_e[0, 1]
        z = s_e[step + 1, 0] - pull * r_e[step + 1, 1]
        z_other = r_e[step + 1, 0] - pull_other * s_e[step + 1, 1]
        x = (z + ratio * z_other) / (1.0 - ratio * ratio_other)
        W[row(levels - 1), :] = x
        return z_other + ratio_other * x, x

    def substitute(c, carry):
        def one(e, beyond, x):
            here = Z[row(e), :] + C[row(e), :] * x
            W[row(e), :] = here
            at = row(e + 1)
            P[at, :] = P[at, :] - H[at, :] * (beyond - here)
            return x, here

        def block(b, carry):
            for u in range(8):
                carry = one((c + 1) * span - 2 - b * 8 - u, *carry)
            return carry

        carry = lax.fori_loop(0, tiles - 1 if c == 0 else tiles, block, carry)
        if c == 0:
            for u in range(7):
                carry = one(6 - u, *carry)
            at = row(0)
            P[at, :] = P[at, :] - H[at, :] * carry[0]
        return carry

    def write_nodes(field, out, c):
        def work(l0, b0):
            for n in range(16):
                out[column_rows(n, l0)] = lanes(field[node_rows(n, l0)], order)

        each_tile(c, work)

    def write_geopotential(c):
        def work(l0, b0):
            for n in range(16):
                value = G[node_rows(n, l0)] + geopotential_rate * W[column_rows(n, l0)]
                o_geo[column_rows(n, l0)] = lanes(value, order)

        each_tile(c, work)

    def write_rows(field, out):
        def go(b, carry):
            for q in range(16):
                at = pl.ds(pl.multiple_of(b * 128 + q * 8, 8), 8)
                out[at, :] = lanes(field[at, :], order)
            return carry

        lax.fori_loop(0, levels // TILE, go, 0)

    stores = []

    def store(src, dst):
        copy = pltpu.make_async_copy(src, dst, store_sem.at[len(stores)])
        copy.start()
        stores.append(copy)

    edge_copy = None
    solved = None
    for step in range(SUBSTEPS):
        uv, w, d, g, m = {}, {}, {}, {}, {}
        for c in reversed(range(CHUNKS)):
            at = sequence[c]
            if step == 0:
                if c == CHUNKS - 1:
                    loaded(lay_in)
                load_mass(at)
                m[c] = send_faces(s_m, r_m, 0, at)
                if c == CHUNKS - 1:
                    loaded(pre_in)
                gather_rows(pre, P, at)
            else:
                solved = substitute(c, solved)
            wind_step(step, at)
            uv[c] = send_faces(s_uv, r_uv, step, at)
        if step == 0:
            loaded(ver_in + geo_in)
        for c in range(CHUNKS):
            at = sequence[c]
            if step == 0:
                gather_rows(ver, W, at)
            vertical_step(step, at)
            w[c] = send_faces(s_w, r_w, step, at)
        if step == 0:
            loaded(zon_in + mer_in)
            for c in reversed(range(CHUNKS)):
                start_winds(sequence[c])
            for c in reversed(range(CHUNKS)):
                arrive(m[c])
                mass_faces(sequence[c])
        for c in reversed(range(CHUNKS)):
            arrive(uv[c])
        for c in range(CHUNKS):
            divergence_step(step, sequence[c])
            d[c] = send_faces(s_d, r_d, step, sequence[c])
        for c in range(CHUNKS):
            if step > 0:
                arrive(late[c])
                geopotential_faces(step - 1, sequence[c])
            geopotential_step(step, sequence[c])
            g[c] = send_faces(s_g, r_g, step, sequence[c])
        late = g
        if step == 0:
            stf_in.wait()
            stiff_copy.wait_recv()
            edge_copy = factor()
        if step == SUBSTEPS - 1:
            for c in range(CHUNKS):
                write_nodes(U, o_zon, c)
                write_nodes(V, o_mer, c)
            store(o_zon, q_zon)
            store(o_mer, q_mer)
        carry = None
        for c in range(CHUNKS):
            arrive(w[c])
            column_faces(W, s_w, r_w, step, sequence[c])
            arrive(d[c])
            column_faces(P, s_d, r_d, step, sequence[c])
            carry = eliminate(step, c, carry)
        if step == 0:
            edge_copy.wait_recv()
        if step == SUBSTEPS - 1:
            for c in range(CHUNKS):
                arrive(late[c])
                geopotential_faces(step, sequence[c])
        carry.wait_recv()
        solved = interface(step)
    for c in reversed(range(CHUNKS)):
        solved = substitute(c, solved)
    write_rows(P, o_pre)
    store(o_pre, q_pre)
    write_rows(W, o_ver)
    store(o_ver, q_ver)
    for c in range(CHUNKS):
        write_geopotential(c)
    store(o_geo, q_geo)
    for copy in started:
        copy.wait_send()
    for copy in stores:
        copy.wait()


def pair_step(
    strips, zonal_wind, meridional_wind, vertical_wind, pressure, geopotential, layer_mass,
    stiffness, elem_order,
):
    levels, nodes, length = zonal_wind.shape
    fields = [
        f.reshape(levels * nodes, length)
        for f in (zonal_wind, meridional_wind, vertical_wind, pressure, geopotential, layer_mass)
    ]
    span = levels // CHUNKS

    def faces(steps, count):
        return [pltpu.VMEM((steps, 2, CHUNKS, count, span, length), jnp.float32)] * 2

    node_major = pltpu.VMEM((nodes, levels, length), jnp.float32)
    level_major = pltpu.VMEM((levels * nodes, length), jnp.float32)
    edges = pltpu.VMEM((SUBSTEPS + 1, 2, nodes, length), jnp.float32)
    copies = 1 + 2 * CHUNKS + SUBSTEPS * 8 * CHUNKS + 1 + SUBSTEPS
    anywhere = pl.BlockSpec(memory_space=pl.ANY)
    outputs = pl.pallas_call(
        functools.partial(fused, strips),
        out_shape=[jax.ShapeDtypeStruct((levels * nodes, length), jnp.float32)] * 5,
        in_specs=[anywhere] * 8,
        out_specs=[anywhere] * 5,
        scratch_shapes=[node_major] * 5
        + [level_major] * 7
        + faces(1, 3)
        + faces(SUBSTEPS, 6)
        + faces(SUBSTEPS, 3)
        + faces(SUBSTEPS, 3)
        + faces(SUBSTEPS, 3)
        + [edges, edges, pltpu.VMEM((levels, nodes // 2, length), jnp.float32)]
        + [level_major] * 6
        + [pltpu.VMEM((levels, nodes // 2, length), jnp.float32)]
        + [pltpu.VMEM((1, length), jnp.int32)]
        + [level_major] * 5
        + [pltpu.SemaphoreType.DMA((copies,)), pltpu.SemaphoreType.DMA((copies,))]
        + [pltpu.SemaphoreType.DMA((14,)), pltpu.SemaphoreType.DMA((5,))],
        compiler_params=pltpu.CompilerParams(
            collective_id=0, has_side_effects=True, vmem_limit_bytes=52 * 1024 * 1024
        ),
        name="acoustic_substeps",
    )(*fields, stiffness, elem_order)
    return tuple(f.reshape(levels, nodes, length) for f in outputs)


def local_step(strips, pair, *arrays):
    levels, nodes, length = arrays[0].shape
    if pair == 2 and strips > 2 and nodes == 16 and length == 128 and levels % (CHUNKS * TILE) == 0:
        return pair_step(strips, *arrays)
    return body(*arrays)


def solution(mesh):
    placed = (
        P("lev", None, "elem"),
        P("lev", None, "elem"),
        P("lev", None, "elem"),
        P("lev", None, "elem"),
        P("lev", None, "elem"),
        P("lev", None, "elem"),
        P(None, "lev", "elem"),
        P("elem", None),
    )
    return jax.shard_map(
        functools.partial(local_step, mesh.shape["elem"], mesh.shape["lev"]),
        mesh=mesh,
        in_specs=placed,
        out_specs=(
            P("lev", None, "elem"),
            P("lev", None, "elem"),
            P("lev", None, "elem"),
            P("lev", None, "elem"),
            P("lev", None, "elem"),
        ),
        check_vma=False,
    )
```

```python
import functools
import math

import jax
import jax.numpy as jnp
import numpy as np
from jax import lax
from jax.experimental import pallas as pl
from jax.experimental.pallas import tpu as pltpu
from jax.sharding import PartitionSpec as P

SUBSTEPS = 3


horizontal_speed = 0.12
drift_first = 0.1
drift_second = 0.06
geopotential_rate = 2.0


def padded(cells, sides, width):
    for axis, dim in sides:
        count = lax.axis_size(axis)
        head = lax.slice_in_dim(cells, 0, width, axis=dim)
        tail = lax.slice_in_dim(cells, cells.shape[dim] - width, cells.shape[dim], axis=dim)
        cells = jnp.concatenate(
            [
                lax.ppermute(tail, axis, [(i, (i + 1) % count) for i in range(count)]),
                cells,
                lax.ppermute(head, axis, [((i + 1) % count, i) for i in range(count)]),
            ],
            axis=dim,
        )
    return cells


def gll_tables():
    points = np.array([-1.0, -1.0 / math.sqrt(5.0), 1.0 / math.sqrt(5.0), 1.0])
    quadrature = np.array([1.0 / 6.0, 5.0 / 6.0, 5.0 / 6.0, 1.0 / 6.0])
    derivative = np.zeros((4, 4))
    for target in range(4):
        for source in range(4):
            if target == source:
                derivative[target, source] = sum(
                    (
                        1.0 / (points[target] - points[other])
                        for other in range(4)
                        if other != target
                    )
                )
            else:
                top_term = math.prod(
                    (points[target] - points[other] for other in range(4) if other != target)
                )
                low_term = math.prod(
                    (points[source] - points[other] for other in range(4) if other != source)
                )
                derivative[target, source] = top_term / (
                    low_term * (points[target] - points[source])
                )
    return (
        jnp.asarray(derivative, jnp.float32),
        jnp.asarray(np.outer(quadrature, quadrature).reshape(16), jnp.float32),
    )


def derivative_along(field, letters, which, derivative):
    result = letters.replace(which, "a")
    return jnp.einsum(
        "a" + which + "," + letters + "->" + result,
        derivative,
        field,
        precision=lax.Precision.HIGHEST,
    )


def assemble(stacked):
    axis_i, axis_j, axis_y = (2, 3, 4)
    left = lax.index_in_dim(stacked, 0, axis_i, keepdims=False)
    right = lax.index_in_dim(stacked, 3, axis_i, keepdims=False)
    faces = jnp.stack([left, right], 0)
    extended = padded(faces, (("elem", 0),), 1)
    left = left + extended[0]
    right = right + extended[3]
    stacked = jnp.concatenate(
        [
            jnp.expand_dims(left, axis_i),
            lax.slice_in_dim(stacked, 1, 3, axis=axis_i),
            jnp.expand_dims(right, axis_i),
        ],
        axis_i,
    )
    lower = lax.index_in_dim(stacked, 0, axis_j, keepdims=False)
    upper = lax.index_in_dim(stacked, 3, axis_j, keepdims=False)
    faces = jnp.stack([lower, upper], 0)
    length = faces.shape[axis_y]
    extended = jnp.concatenate(
        [
            lax.slice_in_dim(faces, length - 1, length, axis=axis_y),
            faces,
            lax.slice_in_dim(faces, 0, 1, axis=axis_y),
        ],
        axis_y,
    )
    lower = lower + lax.slice_in_dim(extended[1], 0, length, axis=axis_y - 1)
    upper = upper + lax.slice_in_dim(extended[0], 2, length + 2, axis=axis_y - 1)
    return jnp.concatenate(
        [
            jnp.expand_dims(lower, axis_j),
            lax.slice_in_dim(stacked, 1, 3, axis=axis_j),
            jnp.expand_dims(upper, axis_j),
        ],
        axis_j,
    )


def lift(field, stride, axis, fill):
    length = field.shape[axis]
    kept = lax.slice_in_dim(field, stride, length, axis=axis)
    padding = jnp.full_like(lax.slice_in_dim(field, 0, stride, axis=axis), fill)
    return jnp.concatenate([kept, padding], axis)


def sink(field, stride, axis, fill):
    length = field.shape[axis]
    kept = lax.slice_in_dim(field, 0, length - stride, axis=axis)
    padding = jnp.full_like(lax.slice_in_dim(field, 0, stride, axis=axis), fill)
    return jnp.concatenate([padding, kept], axis)


def column_step(upward, press, coeff, root, axis):
    rhs = upward - root * 0.5 * (lift(press, 1, axis, 0.0) - sink(press, 1, axis, 0.0))
    lower = -coeff
    upper = -coeff
    middle = 1.0 + 2.0 * coeff
    length = coeff.shape[axis]
    stride = 1
    while stride < length:
        from_below = -lower / sink(middle, stride, axis, 1.0)
        from_above = -upper / lift(middle, stride, axis, 1.0)
        new_lower = from_below * sink(lower, stride, axis, 0.0)
        new_upper = from_above * lift(upper, stride, axis, 0.0)
        middle = (
            middle
            + from_below * sink(upper, stride, axis, 0.0)
            + from_above * lift(lower, stride, axis, 0.0)
        )
        rhs = (
            rhs
            + from_below * sink(rhs, stride, axis, 0.0)
            + from_above * lift(rhs, stride, axis, 0.0)
        )
        lower, upper = (new_lower, new_upper)
        stride = stride * 2
    solved = rhs / middle
    press = press - root * 0.5 * (lift(solved, 1, axis, 0.0) - sink(solved, 1, axis, 0.0))
    return (solved, press)


def substep(state, mass, recip, letters, derivative, vertical):
    zonal, meridional, upward, press, geopot = state
    tendencies = jnp.stack(
        [
            mass * (-horizontal_speed * derivative_along(press, letters, "i", derivative)),
            mass * (-horizontal_speed * derivative_along(press, letters, "j", derivative)),
            mass
            * -(
                drift_first * derivative_along(upward, letters, "i", derivative)
                + drift_second * derivative_along(upward, letters, "j", derivative)
            ),
            mass
            * -(
                drift_first * derivative_along(geopot, letters, "i", derivative)
                + drift_second * derivative_along(geopot, letters, "j", derivative)
            ),
        ],
        0,
    )
    summed = assemble(tendencies)
    zonal = zonal + recip * summed[0]
    meridional = meridional + recip * summed[1]
    upward = upward + recip * summed[2]
    geopot = geopot + recip * summed[3]
    divergence = derivative_along(zonal, letters, "i", derivative) + derivative_along(
        meridional, letters, "j", derivative
    )
    press = press + recip * assemble(jnp.expand_dims(mass * (-horizontal_speed * divergence), 0))[0]
    solved, press = vertical(upward, press)
    geopot = geopot + geopotential_rate * solved
    return (zonal, meridional, solved, press, geopot)


def body(
    zonal_wind,
    meridional_wind,
    vertical_wind,
    pressure,
    geopotential,
    layer_mass,
    stiffness,
    elem_order,
):
    derivative, weights = gll_tables()
    order = elem_order[0]
    length = order.shape[0]
    inverse = jnp.zeros((length,), jnp.int32).at[order].set(jnp.arange(length, dtype=jnp.int32))
    levels = zonal_wind.shape[0]
    fields = [
        jnp.take(field, inverse, axis=2)
        for field in (zonal_wind, meridional_wind, vertical_wind, pressure, geopotential)
    ]
    mass = jnp.take(layer_mass, inverse, axis=2) * weights[None, :, None]
    coeff_grid = jnp.take(stiffness, inverse, axis=2)
    grid_mass = mass.reshape(levels, 4, 4, length)
    recip = 1.0 / assemble(jnp.expand_dims(grid_mass, 0))[0]
    root_grid = jnp.sqrt(coeff_grid)

    def vertical(upward, press):
        stacked = jnp.stack([upward, press], 0).reshape(2, levels, 16, length)
        columns = lax.all_to_all(stacked, "lev", split_axis=2, concat_axis=1, tiled=True)
        solved, press_new = column_step(columns[0], columns[1], coeff_grid, root_grid, 0)
        back = lax.all_to_all(
            jnp.stack([solved, press_new], 0), "lev", split_axis=1, concat_axis=2, tiled=True
        )
        back = back.reshape(2, levels, 4, 4, length)
        return (back[0], back[1])

    state = tuple((field.reshape(levels, 4, 4, length) for field in fields))
    for step in range(SUBSTEPS):
        state = substep(state, grid_mass, recip, "lijy", derivative, vertical)
    results = [field.reshape(levels, 16, length) for field in state]
    outputs = [jnp.take(field, order, axis=2) for field in results]
    return (outputs[0], outputs[1], outputs[2], outputs[3], outputs[4])


CHUNKS = 2
TILE = 8


def derivative_parts():
    points = np.array([-1.0, -1.0 / math.sqrt(5.0), 1.0 / math.sqrt(5.0), 1.0])
    matrix = np.zeros((4, 4))
    for a in range(4):
        for b in range(4):
            if a == b:
                matrix[a, b] = sum(1.0 / (points[a] - points[o]) for o in range(4) if o != a)
            else:
                top = math.prod(points[a] - points[o] for o in range(4) if o != a)
                low = math.prod(points[b] - points[o] for o in range(4) if o != b)
                matrix[a, b] = top / (low * (points[a] - points[b]))
    return matrix


MATRIX = derivative_parts()


def line(f0, f1, f2, f3, scale):
    outer, inner = f0 - f3, f1 - f2
    bend = (f0 + f3) - (f1 + f2)
    out = [None] * 4
    for a in (0, 1):
        m = MATRIX[a] * scale
        odd = float(0.5 * (m[0] - m[3])) * outer + float(0.5 * (m[1] - m[2])) * inner
        even = float(0.5 * (m[0] + m[3])) * bend
        out[a], out[3 - a] = odd + even, odd - even
    return out


def along_i(f, scale):
    out = [None] * 16
    for j in range(4):
        for i, value in enumerate(line(f[j], f[4 + j], f[8 + j], f[12 + j], scale)):
            out[4 * i + j] = value
    return out


def along_j(f, scale):
    out = [None] * 16
    for i in range(4):
        out[4 * i : 4 * i + 4] = line(*f[4 * i : 4 * i + 4], scale)
    return out


def ahead(x):
    return pltpu.roll(x, x.shape[1] - 1, 1)


def behind(x):
    return pltpu.roll(x, 1, 1)


def join_j(f):
    out = list(f)
    for i in range(4):
        shared = f[4 * i + 3] + ahead(f[4 * i])
        out[4 * i + 3] = shared
        out[4 * i] = behind(shared)
    return out


def lanes(x, index):
    return jnp.take_along_axis(x, index, axis=1, mode="promise_in_bounds")


def fused(
    strips,
    h_zon, h_mer, h_ver, h_pre, h_geo, h_lay, h_stf, h_ord,
    q_zon, q_mer, q_ver, q_pre, q_geo,
    U, V, G, M, R, P, W, Z, C, I, H, A,
    s_m, r_m, s_uv, r_uv, s_w, r_w, s_d, r_d, s_g, r_g, s_e, r_e, r_a,
    zon, mer, ver, pre, geo, lay, stf, ord_ref,
    o_zon, o_mer, o_ver, o_pre, o_geo, send_sem, recv_sem, load_sem, store_sem,
):
    levels = U.shape[1]
    span = levels // CHUNKS
    tiles = span // TILE
    me = lax.axis_index("elem")
    lev = lax.axis_index("lev")
    left, right = lax.rem(me + strips - 1, strips), lax.rem(me + 1, strips)
    other = 1 - lev
    sequence = [c + lev * (CHUNKS - 1 - 2 * c) for c in range(CHUNKS)]
    quad = [1.0 / 6.0, 5.0 / 6.0, 5.0 / 6.0, 1.0 / 6.0]
    weights = [quad[n // 4] * quad[n % 4] for n in range(16)]
    started = []
    MESH = pl.DeviceIdType.MESH

    def send(src, dst, target):
        slot = len(started)
        copy = pltpu.make_async_remote_copy(
            src_ref=src, dst_ref=dst, send_sem=send_sem.at[slot], recv_sem=recv_sem.at[slot],
            device_id=target, device_id_type=MESH,
        )
        copy.start()
        started.append(copy)
        return copy

    def send_faces(out, back, step, c):
        return [
            send(out.at[step, 0, c], back.at[step, 0, c], {"elem": left}),
            send(out.at[step, 1, c], back.at[step, 1, c], {"elem": right}),
        ]

    def arrive(copies):
        for copy in copies:
            copy.wait_recv()

    def column_rows(n, l0):
        return (pl.ds(l0 * 16 + n, TILE, stride=16), slice(None))

    def node_rows(n, l0):
        return (n, pl.ds(l0, TILE), slice(None))

    def each_tile(c, work):
        def go(b, carry):
            work(pl.multiple_of(c * span + b * TILE, TILE), pl.multiple_of(b * TILE, TILE))
            return carry

        lax.fori_loop(0, tiles, go, 0)

    def put_faces(buf, step, c, at, b0, f):
        for j in range(3):
            buf[step, 0, c, at + j, pl.ds(b0, TILE), :] = f[j]
            buf[step, 1, c, at + j, pl.ds(b0, TILE), :] = f[12 + j]

    def total_faces(out, back, step, c, at, b0):
        result = {}
        for i, own, theirs in ((0, 0, 1), (3, 1, 0)):
            for j in range(3):
                result[4 * i + j] = (
                    out[step, own, c, at + j, pl.ds(b0, TILE), :]
                    + back[step, theirs, c, at + j, pl.ds(b0, TILE), :]
                )
            result[4 * i + 3] = ahead(result[4 * i])
        return result

    def fetch(src, dst, slot):
        half = dst.shape[0] // 2
        copies = []
        for part in range(2):
            rows = pl.ds(part * half, half)
            copy = pltpu.make_async_copy(src.at[rows], dst.at[rows], load_sem.at[2 * slot + part])
            copy.start()
            copies.append(copy)
        return copies

    def loaded(copies):
        for copy in copies:
            copy.wait()

    order_in = pltpu.make_async_copy(h_ord, ord_ref, load_sem.at[13])
    order_in.start()
    lay_in, pre_in = fetch(h_lay, lay, 0), fetch(h_pre, pre, 1)
    ver_in, geo_in = fetch(h_ver, ver, 2), fetch(h_geo, geo, 3)
    zon_in, mer_in = fetch(h_zon, zon, 4), fetch(h_mer, mer, 5)
    own = pl.ds(pl.multiple_of(lev * levels, 8), levels)
    stf_in = pltpu.make_async_copy(h_stf.at[own], stf, load_sem.at[12])
    stf_in.start()

    barrier = pltpu.get_barrier_semaphore()
    for target in ({"elem": left}, {"elem": right}, {"lev": other}):
        pl.semaphore_signal(barrier, inc=1, device_id=target, device_id_type=MESH)
    pl.semaphore_wait(barrier, 3)

    stiff_copy = send(h_stf.at[pl.ds(pl.multiple_of(other * levels, 8), levels)], r_a, {"lev": other})

    order_in.wait()
    order = jnp.broadcast_to(ord_ref[...], (TILE, ord_ref.shape[1]))
    lane = lax.broadcasted_iota(jnp.int32, order.shape, 1)
    inv = jnp.zeros_like(order)
    for turn in range(order.shape[1]):
        moved = pltpu.roll(order, turn, 1) if turn else order
        source = jnp.where(lane >= turn, lane - turn, lane - turn + order.shape[1])
        inv = jnp.where(moved == lane, source, inv)

    def gather_rows(src, dst, c):
        def go(b, carry):
            for q in range(16):
                at = pl.ds(pl.multiple_of(c * span * 16 + b * 128 + q * 8, 8), 8)
                dst[at, :] = lanes(src[at, :], inv)
            return carry

        lax.fori_loop(0, tiles, go, 0)

    def load_mass(c):
        def work(l0, b0):
            m = [lanes(lay[column_rows(n, l0)], inv) * weights[n] for n in range(16)]
            for n in range(16):
                M[node_rows(n, l0)] = m[n]
            m = join_j(m)
            for n in range(4, 12):
                R[node_rows(n, l0)] = 1.0 / m[n]
            put_faces(s_m, 0, c, 0, b0, m)

        each_tile(c, work)

    def wind_step(step, c):
        def work(l0, b0):
            p = [P[column_rows(n, l0)] for n in range(16)]
            m = [M[node_rows(n, l0)] for n in range(16)]
            for at, field, d in ((0, U, along_i), (3, V, along_j)):
                t = join_j([x * y for x, y in zip(m, d(p, -horizontal_speed))])
                for n in range(4, 12):
                    add = R[node_rows(n, l0)] * t[n]
                    field[node_rows(n, l0)] = add if step == 0 else field[node_rows(n, l0)] + add
                put_faces(s_uv, step, c, at, b0, t)

        each_tile(c, work)

    def start_winds(c):
        def work(l0, b0):
            for src, field in ((zon, U), (mer, V)):
                for n in range(16):
                    value = lanes(src[column_rows(n, l0)], inv)
                    if 4 <= n < 12:
                        value = value + field[node_rows(n, l0)]
                    field[node_rows(n, l0)] = value

        each_tile(c, work)

    def drift(f, m):
        first, second = along_i(f, -drift_first), along_j(f, -drift_second)
        return join_j([k * (x + y) for k, x, y in zip(m, first, second)])

    def vertical_step(step, c):
        def work(l0, b0):
            m = [M[node_rows(n, l0)] for n in range(16)]
            w = [W[column_rows(n, l0)] for n in range(16)]
            for n in range(16):
                if step == 0:
                    G[node_rows(n, l0)] = lanes(geo[column_rows(n, l0)], inv)
                else:
                    G[node_rows(n, l0)] = G[node_rows(n, l0)] + geopotential_rate * w[n]
            t = drift(w, m)
            for n in range(4, 12):
                W[column_rows(n, l0)] = w[n] + R[node_rows(n, l0)] * t[n]
            put_faces(s_w, step, c, 0, b0, t)

        each_tile(c, work)

    def geopotential_step(step, c):
        def work(l0, b0):
            m = [M[node_rows(n, l0)] for n in range(16)]
            g = [G[node_rows(n, l0)] for n in range(16)]
            t = drift(g, m)
            for n in range(4, 12):
                G[node_rows(n, l0)] = g[n] + R[node_rows(n, l0)] * t[n]
            put_faces(s_g, step, c, 0, b0, t)

        each_tile(c, work)

    def mass_faces(c):
        def work(l0, b0):
            for n, total in total_faces(s_m, r_m, 0, c, 0, b0).items():
                R[node_rows(n, l0)] = 1.0 / total

        each_tile(c, work)

    def divergence_step(step, c):
        def work(l0, b0):
            for at, field in ((0, U), (3, V)):
                for n, total in total_faces(s_uv, r_uv, step, c, at, b0).items():
                    field[node_rows(n, l0)] = field[node_rows(n, l0)] + R[node_rows(n, l0)] * total
            m = [M[node_rows(n, l0)] for n in range(16)]
            du = along_i([U[node_rows(n, l0)] for n in range(16)], -horizontal_speed)
            dv = along_j([V[node_rows(n, l0)] for n in range(16)], -horizontal_speed)
            t = join_j([k * (x + y) for k, x, y in zip(m, du, dv)])
            for n in range(4, 12):
                P[column_rows(n, l0)] = P[column_rows(n, l0)] + R[node_rows(n, l0)] * t[n]
            put_faces(s_d, step, c, 0, b0, t)

        each_tile(c, work)

    def column_faces(field, out, back, step, c):
        def work(l0, b0):
            for n, total in total_faces(out, back, step, c, 0, b0).items():
                field[column_rows(n, l0)] = field[column_rows(n, l0)] + R[node_rows(n, l0)] * total

        each_tile(c, work)

    def geopotential_faces(step, c):
        def work(l0, b0):
            for n, total in total_faces(s_g, r_g, step, c, 0, b0).items():
                G[node_rows(n, l0)] = G[node_rows(n, l0)] + R[node_rows(n, l0)] * total

        each_tile(c, work)

    stride = 16 - 32 * lev
    outer = lev * ((levels - 1) * 16)

    def row(e):
        return pl.ds(pl.multiple_of(outer + stride * e, 16), 16)

    side = (1 - 2 * lev).astype(jnp.float32)
    zero = jnp.zeros((16, P.shape[1]), jnp.float32)

    def factor():
        def fill(k, carry):
            mine = lanes(stf[k], inv)
            theirs = lanes(r_a[k], inv)
            top = jnp.where(lev == 0, mine, theirs)
            bottom = jnp.where(lev == 0, theirs, mine)
            both = jnp.concatenate([top, bottom], 0)
            at = pl.ds(pl.multiple_of(k * 16, 16), 16)
            A[at, :] = both
            H[at, :] = jnp.sqrt(both) * (0.5 * side)
            return carry

        lax.fori_loop(0, levels, fill, 0, unroll=4)

        def go(block, ratio):
            for u in range(4):
                at = row(block * 4 + u)
                a = A[at, :]
                turn = 1.0 / (1.0 + 2.0 * a - a * ratio)
                ratio = a * turn
                C[at, :] = ratio
                I[at, :] = turn
            return ratio

        lax.fori_loop(0, levels // 4, go, zero)
        at = row(levels - 1)
        s_e[0, 0] = C[at, :]
        s_e[0, 1] = H[at, :] * I[at, :]
        return send(s_e.at[0], r_e.at[0], {"lev": other})

    def eliminate(step, c, carry):
        def one(e, before, here, after, z):
            at = row(e)
            z = (W[at, :] - H[at, :] * (after - before)) * I[at, :] + C[at, :] * z
            Z[at, :] = z
            return here, after, z

        def block(b, carry):
            before, here, z = carry
            for u in range(8):
                e = c * span + b * 8 + u - 1
                before, here, z = one(e, before, here, P[row(e + 1), :], z)
            return before, here, z

        if c == 0:
            before, here, z = zero, P[row(0), :], zero
            for u in range(7):
                before, here, z = one(u, before, here, P[row(u + 1), :], z)
            carry = (before, here, z)
        carry = lax.fori_loop(1 if c == 0 else 0, tiles, block, carry)
        if c < CHUNKS - 1:
            return carry
        before, here, z = carry
        last, _, z = one(levels - 1, before, here, zero, z)
        s_e[step + 1, 0] = z
        s_e[step + 1, 1] = last
        return send(s_e.at[step + 1], r_e.at[step + 1], {"lev": other})

    def interface(step):
        ratio, pull = s_e[0, 0], s_e[0, 1]
        ratio_other, pull_other = r_e[0, 0], r_e[0, 1]
        z = s_e[step + 1, 0] - pull * r_e[step + 1, 1]
        z_other = r_e[step + 1, 0] - pull_other * s_e[step + 1, 1]
        x = (z + ratio * z_other) / (1.0 - ratio * ratio_other)
        W[row(levels - 1), :] = x
        return z_other + ratio_other * x, x

    def substitute(c, carry):
        def one(e, beyond, x):
            here = Z[row(e), :] + C[row(e), :] * x
            W[row(e), :] = here
            at = row(e + 1)
            P[at, :] = P[at, :] - H[at, :] * (beyond - here)
            return x, here

        def block(b, carry):
            for u in range(8):
                carry = one((c + 1) * span - 2 - b * 8 - u, *carry)
            return carry

        carry = lax.fori_loop(0, tiles - 1 if c == 0 else tiles, block, carry)
        if c == 0:
            for u in range(7):
                carry = one(6 - u, *carry)
            at = row(0)
            P[at, :] = P[at, :] - H[at, :] * carry[0]
        return carry

    def write_nodes(field, out, c):
        def work(l0, b0):
            for n in range(16):
                out[column_rows(n, l0)] = lanes(field[node_rows(n, l0)], order)

        each_tile(c, work)

    def write_geopotential(c):
        def work(l0, b0):
            for n in range(16):
                value = G[node_rows(n, l0)] + geopotential_rate * W[column_rows(n, l0)]
                o_geo[column_rows(n, l0)] = lanes(value, order)

        each_tile(c, work)

    def write_rows(field, out):
        def go(b, carry):
            for q in range(16):
                at = pl.ds(pl.multiple_of(b * 128 + q * 8, 8), 8)
                out[at, :] = lanes(field[at, :], order)
            return carry

        lax.fori_loop(0, levels // TILE, go, 0)

    stores = []

    def store(src, dst):
        copy = pltpu.make_async_copy(src, dst, store_sem.at[len(stores)])
        copy.start()
        stores.append(copy)

    edge_copy = None
    solved = None
    for step in range(SUBSTEPS):
        uv, w, d, g, m = {}, {}, {}, {}, {}
        for c in reversed(range(CHUNKS)):
            at = sequence[c]
            if step == 0:
                if c == CHUNKS - 1:
                    loaded(lay_in)
                load_mass(at)
                m[c] = send_faces(s_m, r_m, 0, at)
                if c == CHUNKS - 1:
                    loaded(pre_in)
                gather_rows(pre, P, at)
            else:
                solved = substitute(c, solved)
            wind_step(step, at)
            uv[c] = send_faces(s_uv, r_uv, step, at)
        if step == 0:
            loaded(ver_in + geo_in)
        for c in range(CHUNKS):
            at = sequence[c]
            if step == 0:
                gather_rows(ver, W, at)
            vertical_step(step, at)
            w[c] = send_faces(s_w, r_w, step, at)
        if step == 0:
            loaded(zon_in + mer_in)
            for c in reversed(range(CHUNKS)):
                start_winds(sequence[c])
            for c in reversed(range(CHUNKS)):
                arrive(m[c])
                mass_faces(sequence[c])
        for c in reversed(range(CHUNKS)):
            arrive(uv[c])
        for c in range(CHUNKS):
            divergence_step(step, sequence[c])
            d[c] = send_faces(s_d, r_d, step, sequence[c])
        for c in range(CHUNKS):
            if step > 0:
                arrive(late[c])
                geopotential_faces(step - 1, sequence[c])
            geopotential_step(step, sequence[c])
            g[c] = send_faces(s_g, r_g, step, sequence[c])
        late = g
        if step == 0:
            stf_in.wait()
            stiff_copy.wait_recv()
            edge_copy = factor()
        if step == SUBSTEPS - 1:
            for c in range(CHUNKS):
                write_nodes(U, o_zon, c)
                write_nodes(V, o_mer, c)
            store(o_zon, q_zon)
            store(o_mer, q_mer)
        carry = None
        for c in range(CHUNKS):
            arrive(w[c])
            column_faces(W, s_w, r_w, step, sequence[c])
            arrive(d[c])
            column_faces(P, s_d, r_d, step, sequence[c])
            carry = eliminate(step, c, carry)
        if step == 0:
            edge_copy.wait_recv()
        if step == SUBSTEPS - 1:
            for c in range(CHUNKS):
                arrive(late[c])
                geopotential_faces(step, sequence[c])
        carry.wait_recv()
        solved = interface(step)
    for c in reversed(range(CHUNKS)):
        solved = substitute(c, solved)
    write_rows(P, o_pre)
    store(o_pre, q_pre)
    write_rows(W, o_ver)
    store(o_ver, q_ver)
    for c in range(CHUNKS):
        write_geopotential(c)
    store(o_geo, q_geo)
    for copy in started:
        copy.wait_send()
    for copy in stores:
        copy.wait()


def pair_step(
    strips, zonal_wind, meridional_wind, vertical_wind, pressure, geopotential, layer_mass,
    stiffness, elem_order,
):
    levels, nodes, length = zonal_wind.shape
    fields = [
        f.reshape(levels * nodes, length)
        for f in (zonal_wind, meridional_wind, vertical_wind, pressure, geopotential, layer_mass)
    ]
    span = levels // CHUNKS

    def faces(steps, count):
        return [pltpu.VMEM((steps, 2, CHUNKS, count, span, length), jnp.float32)] * 2

    node_major = pltpu.VMEM((nodes, levels, length), jnp.float32)
    level_major = pltpu.VMEM((levels * nodes, length), jnp.float32)
    edges = pltpu.VMEM((SUBSTEPS + 1, 2, nodes, length), jnp.float32)
    copies = 1 + 2 * CHUNKS + SUBSTEPS * 8 * CHUNKS + 1 + SUBSTEPS
    anywhere = pl.BlockSpec(memory_space=pl.ANY)
    outputs = pl.pallas_call(
        functools.partial(fused, strips),
        out_shape=[jax.ShapeDtypeStruct((levels * nodes, length), jnp.float32)] * 5,
        in_specs=[anywhere] * 8,
        out_specs=[anywhere] * 5,
        scratch_shapes=[node_major] * 5
        + [level_major] * 7
        + faces(1, 3)
        + faces(SUBSTEPS, 6)
        + faces(SUBSTEPS, 3)
        + faces(SUBSTEPS, 3)
        + faces(SUBSTEPS, 3)
        + [edges, edges, pltpu.VMEM((levels, nodes // 2, length), jnp.float32)]
        + [level_major] * 6
        + [pltpu.VMEM((levels, nodes // 2, length), jnp.float32)]
        + [pltpu.VMEM((1, length), jnp.int32)]
        + [level_major] * 5
        + [pltpu.SemaphoreType.DMA((copies,)), pltpu.SemaphoreType.DMA((copies,))]
        + [pltpu.SemaphoreType.DMA((14,)), pltpu.SemaphoreType.DMA((5,))],
        compiler_params=pltpu.CompilerParams(
            collective_id=0, has_side_effects=True, vmem_limit_bytes=58 * 1024 * 1024
        ),
        name="acoustic_substeps",
    )(*fields, stiffness, elem_order)
    return tuple(f.reshape(levels, nodes, length) for f in outputs)


def local_step(strips, pair, *arrays):
    levels, nodes, length = arrays[0].shape
    if pair == 2 and strips > 2 and nodes == 16 and length == 128 and levels % (CHUNKS * TILE) == 0:
        return pair_step(strips, *arrays)
    return body(*arrays)


def solution(mesh):
    placed = (
        P("lev", None, "elem"),
        P("lev", None, "elem"),
        P("lev", None, "elem"),
        P("lev", None, "elem"),
        P("lev", None, "elem"),
        P("lev", None, "elem"),
        P(None, "lev", "elem"),
        P("elem", None),
    )
    return jax.shard_map(
        functools.partial(local_step, mesh.shape["elem"], mesh.shape["lev"]),
        mesh=mesh,
        in_specs=placed,
        out_specs=(
            P("lev", None, "elem"),
            P("lev", None, "elem"),
            P("lev", None, "elem"),
            P("lev", None, "elem"),
            P("lev", None, "elem"),
        ),
        check_vma=False,
    )
```
